128 devices in a mesh: ctx: 16 (over y, z), tp: 4 (over x), dp: 2 (over core).
Axes of the slice: x: 4, y: 4, z: 4, core: 2. Of those that a mesh axis runs over, the one named last changes fastest.
Arguments:
- queries: bfloat16 [2, 2048, 2048], P('dp', 'ctx', 'tp'), may hold values from -96 to 96
- key_rows: bfloat16 [2, 2048, 2048], P('dp', 'ctx', 'tp'), may hold values from -32 to 32
- value_rows: bfloat16 [2, 2048, 4096], P('dp', 'ctx', 'tp'), may hold values from -6 to 6
- log_decay: float32 [2, 32, 2048], P('dp', 'tp', 'ctx'), may hold values from -0.77 to 0
- write_rate: float32 [2, 32, 2048], P('dp', 'tp', 'ctx'), may hold values from 0.05 to 0.95
- initial_state: float32 [2, 32, 128, 128], P('dp', 'tp'), may hold values from -6 to 6
- final_state_grad: float32 [2, 32, 128, 128], P('dp', 'tp'), may hold values from -6 to 6
- output_matrix: bfloat16 [2048, 4096], P('dp', 'tp'), may hold values from -0.09375 to 0.09375
- output_grad: bfloat16 [2, 2048, 2048], P('dp', 'ctx', 'tp'), may hold values from -6 to 6
Outputs:
- query_grad: bfloat16 [2, 2048, 2048], P('dp', 'ctx', 'tp')
- key_grad: bfloat16 [2, 2048, 2048], P('dp', 'ctx', 'tp')
- value_grad: bfloat16 [2, 2048, 4096], P('dp', 'ctx', 'tp')
- decay_grad: float32 [2, 32, 2048], P('dp', 'tp', 'ctx')
- rate_grad: float32 [2, 32, 2048], P('dp', 'tp', 'ctx')
- weight_grad: float32 [2048, 4096], P('dp', 'tp')
The draws below stay inside these ranges and needn't reach their ends.
All inputs are finite; a program needn't handle non-finite values.
Results may differ from the reference program's by a relative error of at most 0.02.
Values may be sent and summed in bfloat16 or wider, within the bound.
No kernel may reach another device: no remote copies, remote signals or barrier semaphores. Data moves between devices by JAX's collectives and lax.ppermute only.
A program may use at most 128 MiB of HBM per device.

```python
import math
import jax
import jax.numpy as jnp
from jax import lax

D = 2048
HK = 16
HV = 32
DK = 128
DV = 128
BLOCK = 128
TOKENS = 2048
BATCH = 2


def draw_queries(key, part):
    key = jax.random.fold_in(key, 5)
    key_base, key_cols, key_rows_s = jax.random.split(key, 3)
    shape_full = (BATCH, TOKENS, HK, DK)
    base = jax.random.truncated_normal(key_base, -4.0, 4.0, shape_full, jnp.float32)
    columns = jnp.exp(jax.random.uniform(key_cols, (HK, DK), jnp.float32, math.log(0.3), math.log(3.0)))
    multipliers = jnp.exp(jax.random.uniform(key_rows_s, (BATCH, TOKENS, HK, 1), jnp.float32, 0.0, math.log(8.0)))
    return (base * columns * multipliers).reshape(BATCH, TOKENS, HK * DK).astype(jnp.bfloat16)


def draw_key_rows(key, part):
    key = jax.random.fold_in(key, 7)
    key_base, key_cols, key_rows_s = jax.random.split(key, 3)
    shape_full = (BATCH, TOKENS, HK, DK)
    base = jax.random.truncated_normal(key_base, -4.0, 4.0, shape_full, jnp.float32)
    columns = jnp.exp(jax.random.uniform(key_cols, (HK, DK), jnp.float32, math.log(0.01), 0.0))
    multipliers = jnp.exp(jax.random.uniform(key_rows_s, (BATCH, TOKENS, HK, 1), jnp.float32, 0.0, math.log(8.0)))
    return (base * columns * multipliers).reshape(BATCH, TOKENS, HK * DK).astype(jnp.bfloat16)


def draw_log_decay(key, part):
    key = jax.random.fold_in(key, 9)
    key_slow, key_fast, key_rough, key_spots, key_drop = jax.random.split(key, 5)
    slow_share = 0.5
    slow_heads = jax.random.uniform(key_slow, (BATCH, HV, 1), jnp.float32) < slow_share
    fast_rate = jnp.exp(jax.random.uniform(key_fast, (BATCH, HV, 1), jnp.float32, math.log(1.0 / 50.0), math.log(1.0 / 30.0)))
    slow_rate = math.log(2.0) / TOKENS
    channel_decay_speed = jnp.where(slow_heads, slow_rate, fast_rate)
    noise_perturbation = jnp.exp(jax.random.uniform(key_rough, (BATCH, HV, TOKENS), jnp.float32, math.log(0.5), math.log(2.0)))
    flagged_indices = jax.random.randint(key_spots, (BATCH, 1, 1, 3), 0, TOKENS)
    sequence_indices = jnp.arange(TOKENS, dtype=jnp.int32)[None, None, :, None]
    spike_count = jnp.any(sequence_indices == flagged_indices, axis=-1)
    discard_fraction = jax.random.uniform(key_drop, (BATCH, HV, 1), jnp.float32, math.log(0.5), math.log(0.8))
    return -channel_decay_speed * noise_perturbation + jnp.where(spike_count, discard_fraction, 0.0)


def shard_levels(own_key, dims, cuts, least, top_value):
    level, own = 1.0, jax.random.fold_in(own_key, 6)
    for position, blocks in cuts:
        draws = jnp.exp(jax.random.uniform(jax.random.fold_in(own, position), (blocks,), jnp.float32, least / len(cuts), top_value / len(cuts)))
        level = level * jnp.repeat(draws, dims[position] // blocks).reshape([-1 if axis == position else 1 for axis in range(len(dims))])
    return level


def scatter_about(own_key, dims, deviation, reach, shards=(), kind=jnp.bfloat16):
    entries = deviation * jax.random.normal(own_key, dims, jnp.float32)
    if shards:
        entries = entries * shard_levels(own_key, dims, shards, -0.22, 0.18)
    return jnp.clip(entries, -reach, reach).astype(kind)


def setup_inputs(seed: int = 0) -> dict:
    streams_of = jax.random.split(jax.random.key(seed), 10)
    queries = draw_queries(jax.random.fold_in(streams_of[9], 71), 0)
    key_rows = draw_key_rows(jax.random.fold_in(streams_of[9], 71), 0)
    value_rows = scatter_about(streams_of[2], (BATCH, TOKENS, HV * DV), 1.0, 6.0, ((0, 2), (1, 16), (2, 4)))
    log_decay = draw_log_decay(jax.random.fold_in(streams_of[9], 71), 0)
    write_rate = jnp.clip(0.05 + 0.9 * jax.random.uniform(streams_of[4], (BATCH, HV, TOKENS), jnp.float32) ** shard_levels(streams_of[4], (BATCH, HV, TOKENS), ((0, 2), (1, 4), (2, 16)), -0.2, 0.2), 0.05, 0.95)
    initial_state = scatter_about(streams_of[5], (BATCH, HV, DV, DK), 1.0, 6.0, ((0, 2), (1, 4)), jnp.float32)
    final_state_grad = scatter_about(streams_of[6], (BATCH, HV, DV, DK), 1.0, 6.0, ((0, 2), (1, 4)), jnp.float32)
    output_matrix = scatter_about(streams_of[7], (D, HV * DV), (HV * DV) ** -0.5, 0.09375, ((0, 2), (1, 4)))
    output_grad = scatter_about(streams_of[8], (BATCH, TOKENS, D), 1.0, 6.0, ((0, 2), (1, 16), (2, 4)))
    return dict(queries=queries, key_rows=key_rows, value_rows=value_rows, log_decay=log_decay, write_rate=write_rate, initial_state=initial_state, final_state_grad=final_state_grad, output_matrix=output_matrix, output_grad=output_grad)


def contract(form, left, right):
    return jnp.einsum(form, left, right, precision=lax.Precision.HIGHEST)

def low_pairs(form, left, right):
    return jnp.einsum(form, left.astype(jnp.bfloat16), right.astype(jnp.bfloat16), preferred_element_type=jnp.float32)

def unit_rows(matrix):
    return matrix * lax.rsqrt(lax.optimization_barrier(jnp.sum(matrix * matrix, axis=-1, keepdims=True)) + 1e-06)

def prepare(query_raw, key_raw, copies):
    normalized_queries = jnp.repeat(unit_rows(query_raw) * DK ** (-0.5), copies, axis=1)
    keys_n = jnp.repeat(unit_rows(key_raw), copies, axis=1)
    return (normalized_queries, keys_n)

def lower_inverse(strict_part, identity_mat, width):
    power = -strict_part
    result = identity_mat + power
    span = 2
    while span < width:
        power = contract('bhij,bhjk->bhik', power, power)
        result = result + contract('bhij,bhjk->bhik', result, power)
        span = span * 2
    return result

def run_blocks(state, normalized_queries, keys_n, values_h, gates, betas, width):
    batch_size, head_count, length = (normalized_queries.shape[0], normalized_queries.shape[1], normalized_queries.shape[2])
    n_blocks = length // width

    def split_up(tensor):
        shaped = tensor.reshape((batch_size, head_count, n_blocks, width) + tensor.shape[3:])
        return jnp.moveaxis(shaped, 2, 0)
    strict_mask = jnp.tril(jnp.ones((width, width), jnp.float32), -1)
    incl_mask = jnp.tril(jnp.ones((width, width), jnp.float32), 0)
    identity_mat = jnp.eye(width, dtype=jnp.float32)

    def advance(state_now, pieces):
        query_blk, key_blk, value_blk, gate_blk, beta_blk = pieces
        cumul_gate = jnp.cumsum(gate_blk, axis=-1)
        gap_matrix = cumul_gate[..., :, None] - cumul_gate[..., None, :]
        decay_strict = strict_mask * jnp.exp(gap_matrix * strict_mask)
        decay_incl = incl_mask * jnp.exp(gap_matrix * incl_mask)
        growth = jnp.exp(cumul_gate)
        inner_prod = low_pairs('bhik,bhjk->bhij', key_blk, key_blk)
        strict_part = beta_blk[..., :, None] * inner_prod * decay_strict
        known_rhs = beta_blk[..., None] * (value_blk - growth[..., None] * contract('bhck,bhvk->bhcv', key_blk, state_now))
        inverse = lower_inverse(strict_part, identity_mat, width)
        fresh_vals = contract('bhij,bhjv->bhiv', inverse, known_rhs)
        scores = low_pairs('bhik,bhjk->bhij', query_blk, key_blk) * decay_incl
        output = growth[..., None] * contract('bhck,bhvk->bhcv', query_blk, state_now) + contract('bhij,bhjv->bhiv', scores, fresh_vals)
        final_gate = cumul_gate[..., -1:]
        weights = jnp.exp(final_gate - cumul_gate)
        updated = jnp.exp(final_gate)[..., None] * state_now + contract('bhcv,bhck->bhvk', fresh_vals, weights[..., None] * key_blk)
        return (updated, output)
    final_state, outputs = lax.scan(jax.checkpoint(advance), state, (split_up(normalized_queries), split_up(keys_n), split_up(values_h), split_up(gates), split_up(betas)))
    outputs = jnp.moveaxis(outputs, 0, 2).reshape(batch_size, head_count, length, values_h.shape[-1])
    return (final_state, outputs)

def head_group(pieces):
    query_part, key_part, value_part, decay_part, rate_part, state_part, state_grad, grad_part = pieces
    copies = value_part.shape[2]

    def forward(query_in, key_in, value_in, decay_in, rate_in):
        normalized_queries, keys_n = prepare(query_in[:, None], key_in[:, None], copies)
        return run_blocks(state_part, normalized_queries, keys_n, jnp.moveaxis(value_in, 2, 1), decay_in, rate_in, BLOCK)
    primal, pull_back = jax.vjp(forward, query_part.astype(jnp.float32), key_part.astype(jnp.float32), value_part.astype(jnp.float32), decay_part, rate_part)
    grads = pull_back((state_grad, jnp.moveaxis(grad_part, 2, 1)))
    return (primal[1],) + tuple(grads)

def reference(queries, key_rows, value_rows, log_decay, write_rate, initial_state, final_state_grad, output_matrix, output_grad):
    copies = HV // HK
    flat_grad = output_grad.reshape(BATCH * TOKENS, D)
    head_grad = jnp.dot(flat_grad, output_matrix, preferred_element_type=jnp.float32)
    head_grad = head_grad.reshape(BATCH, TOKENS, HK, copies, DV)
    stacked = (jnp.moveaxis(queries.reshape(BATCH, TOKENS, HK, DK), 2, 0), jnp.moveaxis(key_rows.reshape(BATCH, TOKENS, HK, DK), 2, 0), jnp.moveaxis(value_rows.reshape(BATCH, TOKENS, HK, copies, DV), 2, 0), jnp.moveaxis(log_decay.reshape(BATCH, HK, copies, TOKENS), 1, 0), jnp.moveaxis(write_rate.reshape(BATCH, HK, copies, TOKENS), 1, 0), jnp.moveaxis(initial_state.reshape(BATCH, HK, copies, DV, DK), 1, 0), jnp.moveaxis(final_state_grad.reshape(BATCH, HK, copies, DV, DK), 1, 0), jnp.moveaxis(head_grad, 2, 0))
    outputs, query_g, key_g, value_g, decay_g, rate_g = lax.map(head_group, stacked)
    heads_low = jnp.transpose(outputs, (1, 3, 0, 2, 4)).reshape(BATCH * TOKENS, HV * DV).astype(jnp.bfloat16)
    weight_grad = lax.dot_general(flat_grad, heads_low, (((0,), (0,)), ((), ())), preferred_element_type=jnp.float32)
    weight_grad = weight_grad * (BATCH * TOKENS) ** (-0.5)
    query_grad = jnp.transpose(query_g, (1, 2, 0, 3)).reshape(BATCH, TOKENS, HK * DK).astype(jnp.bfloat16)
    key_grad = jnp.transpose(key_g, (1, 2, 0, 3)).reshape(BATCH, TOKENS, HK * DK).astype(jnp.bfloat16)
    value_grad = jnp.transpose(value_g, (1, 2, 0, 3, 4)).reshape(BATCH, TOKENS, HV * DV).astype(jnp.bfloat16)
    decay_grad = jnp.moveaxis(decay_g, 0, 1).reshape(BATCH, HV, TOKENS)
    rate_grad = jnp.moveaxis(rate_g, 0, 1).reshape(BATCH, HV, TOKENS)
    return (query_grad, key_grad, value_grad, decay_grad, rate_grad, weight_grad)
```

```python
import functools

import jax
import jax.numpy as jnp
from jax import lax
from jax.experimental import pallas as pl
from jax.experimental.pallas import tpu as pltpu
from jax.sharding import PartitionSpec as P

DK = 128
DV = 128
BLOCK = 128
HALF = DV // 2
F32 = jnp.float32
BF16 = jnp.bfloat16
QSCALE = DK ** (-0.5)

NN = (((1,), (0,)), ((), ()))
NT = (((1,), (1,)), ((), ()))
TN = (((0,), (0,)), ((), ()))


def mm(a, b, dims=NN):
    return lax.dot_general(a.astype(BF16), b.astype(BF16), dims, preferred_element_type=F32)


def split(a):
    high = a.astype(BF16)
    return high, (a - high.astype(F32)).astype(BF16)


def mm3(a, b, dims=NN):
    (ah, al), (bh, bl) = a, b
    dot = functools.partial(lax.dot_general, dimension_numbers=dims, preferred_element_type=F32)
    return dot(ah, bh) + (dot(ah, bl) + dot(al, bh))


def exact(a, b):
    return lax.dot_general(
        a, b, NN, precision=lax.Precision.HIGHEST, preferred_element_type=F32
    )


def iotas():
    row = lax.broadcasted_iota(jnp.int32, (BLOCK, BLOCK), 0)
    col = lax.broadcasted_iota(jnp.int32, (BLOCK, BLOCK), 1)
    return row, col


def unit_rows(rows):
    scale = lax.rsqrt(jnp.sum(rows * rows, axis=-1, keepdims=True) + 1e-06)
    return rows * scale, scale


def gate_columns(gates, row, col):
    cumul = exact(gates, (row <= col).astype(F32))
    columns = cumul.T
    last = columns[BLOCK - 1 : BLOCK, :]
    return cumul, columns, jnp.exp(columns), jnp.exp(last - columns), jnp.exp(last)


def decays(cumul, columns, h, strict):
    gap = columns[:, h : h + 1] - cumul[h : h + 1, :]
    return jnp.where(strict, jnp.exp(jnp.where(strict, gap, 0.0)), 0.0)


def unit_lower_inverses(parts, row, col):
    ident = (row == col).astype(F32)
    found = None
    size = 1
    while size < BLOCK:
        off = (row // (2 * size) == col // (2 * size)) & (row // size != col // size)
        offs = [jnp.where(off, a, 0.0) for a in parts]
        if size == 1:
            found = [ident - a for a in offs]
        else:
            halves = [split(t) for t in found]
            inner = [mm3(t, split(a)) for t, a in zip(halves, offs)]
            found = [t - mm3(split(x), s) for t, x, s in zip(found, inner, halves)]
        size *= 2
    return found


def local_maps(q_ref, k_ref, v_ref, g_ref, b_ref, pay_ref, t_ref, wm_ref, u0_ref, qe_ref, o0_ref):
    heads = g_ref.shape[1]
    copies = heads * DK // q_ref.shape[2]
    row, col = iotas()
    strict = row > col
    ident = (row == col).astype(F32)
    cumul, columns, growth, weight, ends = gate_columns(g_ref[0], row, col)
    betas = b_ref[0].T
    qhat, khat, pair_k, pair_q = [], [], [], []
    for j in range(heads // copies):
        cut = slice(j * DK, (j + 1) * DK)
        qn = unit_rows(q_ref[0, :, cut].astype(F32))[0] * QSCALE
        kn = unit_rows(k_ref[0, :, cut].astype(F32))[0]
        qhat.append(qn)
        khat.append(kn)
        pair_k.append(mm(kn, kn, NT))
        pair_q.append(mm(qn, kn, NT))
    decay = [decays(cumul, columns, h, strict) for h in range(heads)]
    beta = [betas[:, h : h + 1] for h in range(heads)]
    parts = [beta[h] * pair_k[h // copies] * decay[h] for h in range(heads)]
    inverse = unit_lower_inverses(parts, row, col)
    for h in range(heads):
        j = h // copies
        grow = growth[:, h : h + 1]
        value = v_ref[0, :, h * DV : (h + 1) * DV].astype(F32)
        t = split(inverse[h])
        wm = mm3(t, split((beta[h] * grow) * khat[j]))
        u0 = mm3(t, split(beta[h] * value))
        kw = split(weight[:, h : h + 1] * khat[j])
        step = ends[:, h : h + 1] * ident - mm3(split(wm), kw, TN)
        write = mm3(split(u0), kw, TN).astype(BF16)
        scores = pair_q[j] * (decay[h] + ident)
        t_ref[h] = t[0]
        wm_ref[h] = wm.astype(BF16)
        u0_ref[h] = u0.astype(BF16)
        qe_ref[h] = (grow * qhat[j] - mm(scores, wm)).astype(BF16)
        o0_ref[h] = mm(scores, u0).astype(BF16)
        step = step.astype(BF16)
        for half in range(2):
            pay_ref[2 * h + half, 0:DK] = step
            pay_ref[2 * h + half, DK : DK + HALF] = write[half * HALF : (half + 1) * HALF]


def head_grads(d_ref, grad_ref, own_ref, other_ref, qe_ref, pay_ref, hg_ref):
    d = d_ref[0]
    parts = grad_ref.shape[0] // 2
    wide = grad_ref.shape[2]
    total = jnp.zeros((BLOCK, own_ref.shape[1]), F32)
    for i in range(parts):
        cut = slice(i * wide, (i + 1) * wide)
        total += mm(grad_ref[parts * d + i], own_ref[cut, :])
        total += mm(grad_ref[parts * (1 - d) + i], other_ref[cut, :])
    total = total.astype(BF16)
    hg_ref[...] = total
    for h in range(qe_ref.shape[0]):
        back = mm(total[:, h * DV : (h + 1) * DV], qe_ref[h], TN).astype(BF16)
        for half in range(2):
            pay_ref[2 * h + half] = back[half * HALF : (half + 1) * HALF]


def chain(x_ref, l_ref, s0_ref, g1_ref, y_ref):
    blocks = x_ref.shape[0]

    def times(state, step, dims):
        out = mm(jnp.concatenate(split(state), axis=0), step, dims)
        return out[:HALF] + out[HALF:]

    state, back = s0_ref[...], g1_ref[...]
    for c in range(blocks):
        e = blocks - 1 - c
        y_ref[c, 0:HALF] = state.astype(BF16)
        y_ref[e, HALF:] = back.astype(BF16)
        if c < blocks - 1:
            state = times(state, x_ref[c, 0:DK], NN) + x_ref[c, DK : DK + HALF].astype(F32)
            back = times(back, x_ref[e, 0:DK], NT) + l_ref[e].astype(F32)


def state_of(y_ref, h, low):
    return jnp.concatenate(
        [y_ref[2 * h, low : low + HALF], y_ref[2 * h + 1, low : low + HALF]], axis=0
    )


def outputs(qe_ref, o0_ref, y_ref, o_ref):
    for h in range(qe_ref.shape[0]):
        out = o0_ref[h].astype(F32) + mm(qe_ref[h], state_of(y_ref, h, 0), NT)
        o_ref[:, h * DV : (h + 1) * DV] = out.astype(BF16)


def gradients(
    q_ref, k_ref, v_ref, g_ref, b_ref, t_ref, wm_ref, u0_ref, hg_ref, y_ref,
    dq_ref, dk_ref, dv_ref, dg_ref, db_ref,
):
    heads = g_ref.shape[1]
    copies = heads * DK // q_ref.shape[2]
    row, col = iotas()
    strict = row > col
    incl = row >= col
    ident = (row == col).astype(F32)
    cumul, columns, growth, weight, ends = gate_columns(g_ref[0], row, col)
    betas = b_ref[0].T
    lane = lax.broadcasted_iota(jnp.int32, (BLOCK, heads), 1)
    level = lax.broadcasted_iota(jnp.int32, (heads, BLOCK), 0)
    cumul_g = jnp.zeros((BLOCK, heads), F32)
    beta_g = jnp.zeros((BLOCK, heads), F32)
    across = jnp.zeros((heads, BLOCK), F32)
    for j in range(heads // copies):
        cut = slice(j * DK, (j + 1) * DK)
        qn, q_scale = unit_rows(q_ref[0, :, cut].astype(F32))
        khat, k_scale = unit_rows(k_ref[0, :, cut].astype(F32))
        qhat = qn * QSCALE
        qlow, klow = qhat.astype(BF16), khat.astype(BF16)
        pair_k = mm(klow, klow, NT)
        pair_q = mm(qlow, klow, NT)
        qhat_g = jnp.zeros((BLOCK, DK), F32)
        khat_g = jnp.zeros((BLOCK, DK), F32)
        for h in range(j * copies, (j + 1) * copies):
            cut_v = slice(h * DV, (h + 1) * DV)
            decay = decays(cumul, columns, h, strict)
            grow, keep, beta = growth[:, h : h + 1], weight[:, h : h + 1], betas[:, h : h + 1]
            value = v_ref[0, :, cut_v].astype(F32)
            state, back = state_of(y_ref, h, 0), state_of(y_ref, h, HALF)
            out_g = hg_ref[:, cut_v]
            decay_in = decay + ident
            scores = pair_q * decay_in
            fresh = (u0_ref[h].astype(F32) - mm(wm_ref[h], state, NT)).astype(BF16)
            fresh_g = mm(scores, out_g, TN) + mm(keep * khat, back, NT)
            rhs_g = mm(t_ref[h], fresh_g, TN)
            rhs_low = rhs_g.astype(BF16)
            read_q = mm(out_g, state)
            read_k = mm(rhs_low, state)
            scores_g = mm(out_g, fresh, NT)
            part_g = jnp.where(strict, -mm(rhs_low, fresh, NT), 0.0) * decay
            pair_qg = (scores_g * decay_in).astype(BF16)
            pair_kg = (part_g * beta).astype(BF16)
            kept_g = mm(fresh, back)
            part_k = part_g * pair_k
            gaps = scores_g * scores + part_k * beta
            low_q = mm(pair_qg, klow).astype(BF16).astype(F32)
            low_k = mm(pair_qg, qlow, TN) + mm(pair_kg, klow) + mm(pair_kg, klow, TN)
            qhat_g += grow * read_q + low_q
            khat_g += keep * kept_g - (beta * grow) * read_k + low_k.astype(BF16).astype(F32)
            dv_ref[0, :, cut_v] = (beta * rhs_g).astype(BF16)
            read_sum = jnp.sum(read_k * khat, axis=1, keepdims=True)
            beta_col = jnp.sum(rhs_g * value + part_k, axis=1, keepdims=True) - grow * read_sum
            kept_sum = jnp.sum(kept_g * khat, axis=1, keepdims=True) * keep
            grow_g = jnp.sum(read_q * qhat, axis=1, keepdims=True) - beta * read_sum
            cumul_col = grow_g * grow + jnp.sum(gaps, axis=1, keepdims=True) - kept_sum
            whole = jnp.sum(back.astype(F32) * state.astype(F32)) * ends[:, h : h + 1]
            at_end = jnp.sum(kept_sum, axis=0, keepdims=True) + whole
            cumul_col += jnp.where(row[:, 0:1] == BLOCK - 1, at_end, 0.0)
            cumul_g = jnp.where(lane == h, cumul_col, cumul_g)
            beta_g = jnp.where(lane == h, beta_col, beta_g)
            across = jnp.where(level == h, jnp.sum(gaps, axis=0, keepdims=True), across)
        q_along = jnp.sum(qn * qhat_g, axis=1, keepdims=True)
        k_along = jnp.sum(khat * khat_g, axis=1, keepdims=True)
        dq_ref[0, :, cut] = ((q_scale * QSCALE) * (qhat_g - qn * q_along)).astype(BF16)
        dk_ref[0, :, cut] = (k_scale * (khat_g - khat * k_along)).astype(BF16)
    db_ref[0] = beta_g.T
    dg_ref[0] = exact(cumul_g.T - across, (row >= col).astype(F32))


def call(kernel, outs, *args, flops=0, scalars=0):
    size = sum(a.size * a.dtype.itemsize for a in args)
    size += sum(o.size * o.dtype.itemsize for o in outs)
    smem = [pl.BlockSpec(memory_space=pltpu.SMEM)] * scalars
    vmem = [pl.BlockSpec(memory_space=pltpu.VMEM)] * (len(args) - scalars)
    return pl.pallas_call(
        kernel,
        out_shape=outs,
        in_specs=smem + vmem,
        out_specs=[pl.BlockSpec(memory_space=pltpu.VMEM)] * len(outs),
        compiler_params=pltpu.CompilerParams(vmem_limit_bytes=48 * 2**20),
        cost_estimate=pl.CostEstimate(flops=flops, bytes_accessed=size, transcendentals=0),
    )(*args)


def shape(dims, dtype):
    return jax.ShapeDtypeStruct(dims, dtype)


def body(
    queries, key_rows, value_rows, log_decay, write_rate,
    initial_state, final_state_grad, output_matrix, output_grad,
):
    heads = log_decay.shape[1]
    blocks = lax.axis_size("ctx")
    feats = lax.axis_size("tp")
    here, core = lax.axis_index("ctx"), lax.axis_index("dp")
    rows = output_matrix.shape[0]
    swap = [(0, 1), (1, 0)]
    square = (heads, BLOCK, DK)
    unit = 2 * BLOCK**3 * heads

    with jax.named_scope("other_rows"):
        other_matrix = lax.ppermute(output_matrix, "dp", swap)
    with jax.named_scope("gather_grad"):
        gathered = lax.all_to_all(
            jnp.broadcast_to(output_grad, (feats,) + output_grad.shape[1:]), "tp", 0, 0, tiled=True
        )
    with jax.named_scope("local_maps"):
        maps, t, wm, u0, qe, o0 = call(
            local_maps,
            [shape((blocks, DK + HALF, DK), BF16)] + [shape(square, BF16)] * 5,
            queries, key_rows, value_rows, log_decay, write_rate,
            flops=50 * unit,
        )
    with jax.named_scope("head_grads"):
        backs, head_grad = call(
            head_grads,
            [shape((blocks, HALF, DK), BF16), shape((BLOCK, heads * DV), BF16)],
            core.reshape(1), gathered, output_matrix, other_matrix, qe,
            flops=18 * unit, scalars=1,
        )
    with jax.named_scope("send_maps"):
        maps_in = lax.all_to_all(maps, "ctx", 0, 0, tiled=True)
        backs_in = lax.all_to_all(backs, "ctx", 0, 0, tiled=True)
    with jax.named_scope("chain"):
        first = lax.dynamic_index_in_dim(
            initial_state.reshape(blocks, HALF, DK), here, 0, keepdims=False
        )
        last = lax.dynamic_index_in_dim(
            final_state_grad.reshape(blocks, HALF, DK), here, 0, keepdims=False
        )
        states, = call(
            chain, [shape((blocks, 2 * HALF, DK), BF16)], maps_in, backs_in, first, last,
            flops=4 * unit,
        )
    with jax.named_scope("return_states"):
        states = lax.all_to_all(states, "ctx", 0, 0, tiled=True)
    with jax.named_scope("outputs"):
        heads_low, = call(
            outputs, [shape((BLOCK, heads * DV), BF16)], qe, o0, states, flops=unit
        )
    with jax.named_scope("projection"):
        half = feats // 2
        mine = lax.dynamic_slice_in_dim(gathered, half * core, half, 0)
        theirs = lax.dynamic_slice_in_dim(gathered, half * (1 - core), half, 0)
        theirs = lax.ppermute(theirs, "dp", swap)
        other_low = lax.ppermute(heads_low, "dp", swap)

        def wide(parts):
            return jnp.moveaxis(parts, 0, 1).reshape(BLOCK, rows)

        grads = jnp.concatenate([wide(mine), wide(theirs)], axis=0)
        lows = jnp.concatenate([heads_low, other_low], axis=0)
        partial = lax.dot_general(grads, lows, TN, preferred_element_type=F32).astype(BF16)
        pieces = lax.all_to_all(
            partial.reshape(blocks, rows // blocks, heads * DV), "ctx", 0, 0, tiled=True
        )
        piece = jnp.sum(pieces.astype(F32), axis=0)
        piece = piece * float(BLOCK * blocks * lax.axis_size("dp")) ** (-0.5)
        spread = jnp.broadcast_to(piece.astype(BF16), (blocks,) + piece.shape)
        total = lax.all_to_all(spread, "ctx", 0, 0, tiled=True)
        weight_grad = total.reshape(rows, heads * DV).astype(F32)
    with jax.named_scope("gradients"):
        query_g, key_g, value_g, decay_g, rate_g = call(
            gradients,
            [
                shape(queries.shape, BF16),
                shape(key_rows.shape, BF16),
                shape(value_rows.shape, BF16),
                shape(log_decay.shape, F32),
                shape(write_rate.shape, F32),
            ],
            queries, key_rows, value_rows, log_decay, write_rate,
            t, wm, u0, head_grad, states,
            flops=17 * unit,
        )
    return (query_g, key_g, value_g, decay_g, rate_g, weight_grad)


def solution(mesh):
    rows = P("dp", "ctx", "tp")
    gates = P("dp", "tp", "ctx")
    state = P("dp", "tp", None, None)
    return jax.shard_map(
        body,
        mesh=mesh,
        in_specs=(rows, rows, rows, gates, gates, state, state, P("dp", "tp"), rows),
        out_specs=(rows, rows, rows, gates, gates, P("dp", "tp")),
        check_vma=False,
    )
```

```python
import functools
import math

import jax
import jax.numpy as jnp
from jax import lax
from jax.experimental import pallas as pl
from jax.experimental.pallas import tpu as pltpu
from jax.sharding import PartitionSpec as P

DK = 128
DV = 128
BLOCK = 128
HALF = DV // 2
F32 = jnp.float32
BF16 = jnp.bfloat16
QSCALE = DK ** (-0.5)

NN = (((1,), (0,)), ((), ()))
NT = (((1,), (1,)), ((), ()))
TN = (((0,), (0,)), ((), ()))


def mm(a, b, dims=NN):
    return lax.dot_general(a.astype(BF16), b.astype(BF16), dims, preferred_element_type=F32)


def split(a):
    high = a.astype(BF16)
    return high, (a - high.astype(F32)).astype(BF16)


def mm3(a, b, dims=NN):
    (ah, al), (bh, bl) = a, b
    dot = functools.partial(lax.dot_general, dimension_numbers=dims, preferred_element_type=F32)
    return dot(ah, bh) + (dot(ah, bl) + dot(al, bh))


def exact(a, b):
    return lax.dot_general(
        a, b, NN, precision=lax.Precision.HIGHEST, preferred_element_type=F32
    )


def iotas():
    row = lax.broadcasted_iota(jnp.int32, (BLOCK, BLOCK), 0)
    col = lax.broadcasted_iota(jnp.int32, (BLOCK, BLOCK), 1)
    return row, col


def unit_rows(rows):
    scale = lax.rsqrt(jnp.sum(rows * rows, axis=-1, keepdims=True) + 1e-06)
    return rows * scale, scale


def gate_columns(gates, row, col):
    cumul = exact(gates, (row <= col).astype(F32))
    columns = cumul.T
    last = columns[BLOCK - 1 : BLOCK, :]
    return cumul, columns, jnp.exp(columns), jnp.exp(last - columns), jnp.exp(last)


def decays(cumul, columns, h, strict):
    gap = columns[:, h : h + 1] - cumul[h : h + 1, :]
    return jnp.where(strict, jnp.exp(jnp.where(strict, gap, 0.0)), 0.0)


def unit_lower_inverses(parts, row, col):
    ident = (row == col).astype(F32)
    found = None
    size = 1
    while size < BLOCK:
        off = (row // (2 * size) == col // (2 * size)) & (row // size != col // size)
        offs = [jnp.where(off, a, 0.0) for a in parts]
        if size == 1:
            found = [ident - a for a in offs]
        else:
            halves = [split(t) for t in found]
            inner = [mm3(t, split(a)) for t, a in zip(halves, offs)]
            found = [t - mm3(split(x), s) for t, x, s in zip(found, inner, halves)]
        size *= 2
    return found


def local_maps(q_ref, k_ref, v_ref, g_ref, b_ref, pay_ref, t_ref, wm_ref, u0_ref, qe_ref, o0_ref):
    heads = g_ref.shape[1]
    copies = heads * DK // q_ref.shape[2]
    row, col = iotas()
    strict = row > col
    ident = (row == col).astype(F32)
    cumul, columns, growth, weight, ends = gate_columns(g_ref[0], row, col)
    betas = b_ref[0].T
    qhat, khat, pair_k, pair_q = [], [], [], []
    for j in range(heads // copies):
        cut = slice(j * DK, (j + 1) * DK)
        qn = unit_rows(q_ref[0, :, cut].astype(F32))[0] * QSCALE
        kn = unit_rows(k_ref[0, :, cut].astype(F32))[0]
        qhat.append(qn)
        khat.append(kn)
        pair_k.append(mm(kn, kn, NT))
        pair_q.append(mm(qn, kn, NT))
    decay = [decays(cumul, columns, h, strict) for h in range(heads)]
    beta = [betas[:, h : h + 1] for h in range(heads)]
    parts = [beta[h] * pair_k[h // copies] * decay[h] for h in range(heads)]
    inverse = unit_lower_inverses(parts, row, col)
    for h in range(heads):
        j = h // copies
        grow = growth[:, h : h + 1]
        value = v_ref[0, :, h * DV : (h + 1) * DV].astype(F32)
        t = split(inverse[h])
        wm = mm3(t, split((beta[h] * grow) * khat[j]))
        u0 = mm3(t, split(beta[h] * value))
        kw = split(weight[:, h : h + 1] * khat[j])
        step = ends[:, h : h + 1] * ident - mm3(split(wm), kw, TN)
        write = mm3(split(u0), kw, TN).astype(BF16)
        scores = pair_q[j] * (decay[h] + ident)
        t_ref[h] = t[0]
        wm_ref[h] = wm.astype(BF16)
        u0_ref[h] = u0.astype(BF16)
        qe_ref[h] = (grow * qhat[j] - mm(scores, wm)).astype(BF16)
        o0_ref[h] = mm(scores, u0).astype(BF16)
        step = step.astype(BF16)
        for half in range(2):
            pay_ref[2 * h + half, 0:DK] = step
            pay_ref[2 * h + half, DK : DK + HALF] = write[half * HALF : (half + 1) * HALF]


def head_grads(
    at_ref, g0_ref, g1_ref, g2_ref, g3_ref, own_hbm, other_ref, qe_hbm, pay_in,
    pay_ref, hg_ref, mine_ref, theirs_ref, all_ref, own_ref, qe_ref, back_ref, in_sems, out_sem,
):
    fetch = pltpu.make_async_copy(own_hbm, own_ref, in_sems.at[0])
    fetch_qe = pltpu.make_async_copy(qe_hbm, qe_ref, in_sems.at[1])
    fetch.start()
    fetch_qe.start()
    core, here = at_ref[0], at_ref[1]
    feats, wide = all_ref.shape[0], all_ref.shape[2]
    parts = feats // 2
    for k, ref in enumerate((g0_ref, g1_ref, g2_ref, g3_ref)):
        all_ref[lax.rem(here + k, feats)] = ref[0]
    total = jnp.zeros((BLOCK, own_ref.shape[1]), F32)
    for i in range(parts):
        cut = slice(i * wide, (i + 1) * wide)
        theirs = all_ref[parts * (1 - core) + i]
        total += mm(theirs, other_ref[cut, :])
        theirs_ref[:, cut] = theirs
    fetch.wait()
    for i in range(parts):
        cut = slice(i * wide, (i + 1) * wide)
        mine = all_ref[parts * core + i]
        total += mm(mine, own_ref[cut, :])
        mine_ref[:, cut] = mine
    total = total.astype(BF16)
    hg_ref[...] = total
    fetch_qe.wait()
    for h in range(qe_ref.shape[0]):
        back = mm(total[:, h * DV : (h + 1) * DV], qe_ref[h], TN).astype(BF16)
        for half in range(2):
            back_ref[2 * h + half] = back[half * HALF : (half + 1) * HALF]
    put = pltpu.make_async_copy(back_ref, pay_ref.at[:, pl.ds(DK + HALF, HALF)], out_sem)
    put.start()
    put.wait()


def chain(maps_ref, first_ref, last_ref, out_ref, kept_ref, sems):
    blocks = maps_ref.shape[0]
    copies = []

    def times(state, step, dims):
        out = mm(jnp.concatenate(split(state), axis=0), step, dims)
        return out[:HALF] + out[HALF:]

    def send(value, c, side):
        rows = pl.ds(side * HALF, HALF)
        kept_ref[c, rows] = value.astype(BF16)
        copy = pltpu.make_async_copy(kept_ref.at[c, rows], out_ref.at[c, rows], sems.at[c, side])
        copy.start()
        copies.append(copy)

    state, back = first_ref[...], last_ref[...]
    for c in range(blocks):
        e = blocks - 1 - c
        send(state, c, 0)
        send(back, e, 1)
        if c < blocks - 1:
            write = maps_ref[c, DK : DK + HALF].astype(F32)
            read = maps_ref[e, DK + HALF :].astype(F32)
            state = times(state, maps_ref[c, 0:DK], NN) + write
            back = times(back, maps_ref[e, 0:DK], NT) + read
    for copy in copies:
        copy.wait()


def projection(mine_ref, theirs_ref, low_ref, other_ref, out_ref, kept_ref, sems):
    blocks, piece = out_ref.shape[0], out_ref.shape[1]
    parts = sems.shape[0]
    some = blocks // parts
    copies = []
    for p in range(parts):
        cut = slice(p * some * piece, (p + 1) * some * piece)
        total = mm(mine_ref[:, cut], low_ref[...], TN) + mm(theirs_ref[:, cut], other_ref[...], TN)
        total = total.astype(BF16)
        for c in range(some):
            kept_ref[p * some + c] = total[c * piece : (c + 1) * piece]
        at = pl.ds(p * some, some)
        copies.append(pltpu.make_async_copy(kept_ref.at[at], out_ref.at[at], sems.at[p]))
        copies[-1].start()
    for copy in copies:
        copy.wait()


def reduce_spread(scale, pieces_ref, out_ref, sum_ref, sems):
    blocks, rows = out_ref.shape[:2]
    parts = sems.shape[1]
    copies = []
    for p in range(parts):
        at = pl.ds(p * (rows // parts), rows // parts)
        total = pieces_ref[0, at].astype(F32)
        for c in range(1, blocks):
            total += pieces_ref[c, at].astype(F32)
        sum_ref[at] = (total * scale).astype(BF16)
        for c in range(blocks):
            copy = pltpu.make_async_copy(sum_ref.at[at], out_ref.at[c, at], sems.at[c, p])
            copy.start()
            copies.append(copy)
    for copy in copies:
        copy.wait()


def widen(in_ref, out_ref, kept_ref, sems):
    parts = sems.shape[0]
    step = in_ref.shape[0] // parts
    copies = []
    for p in range(parts):
        at = pl.ds(p * step, step)
        kept_ref[at, :] = in_ref[at, :].astype(F32)
        copies.append(pltpu.make_async_copy(kept_ref.at[at], out_ref.at[at], sems.at[p]))
        copies[-1].start()
    for copy in copies:
        copy.wait()


def halves_of(ref, h, low):
    rows = slice(low, low + HALF)
    return jnp.concatenate([ref[2 * h, rows], ref[2 * h + 1, rows]], axis=0)


def outputs(qe_ref, o0_ref, y_ref, o_ref):
    for h in range(qe_ref.shape[0]):
        out = o0_ref[h].astype(F32) + mm(qe_ref[h], halves_of(y_ref, h, 0), NT)
        o_ref[:, h * DV : (h + 1) * DV] = out.astype(BF16)


def gradients(
    q_ref, k_ref, v_ref, g_ref, b_ref, t_ref, wm_ref, u0_ref, hg_ref, y_ref,
    dq_ref, dk_ref, dv_ref, dg_ref, db_ref,
):
    heads = g_ref.shape[1]
    copies = heads * DK // q_ref.shape[2]
    row, col = iotas()
    strict = row > col
    incl = row >= col
    ident = (row == col).astype(F32)
    cumul, columns, growth, weight, ends = gate_columns(g_ref[0], row, col)
    betas = b_ref[0].T
    lane = lax.broadcasted_iota(jnp.int32, (BLOCK, heads), 1)
    level = lax.broadcasted_iota(jnp.int32, (heads, BLOCK), 0)
    cumul_g = jnp.zeros((BLOCK, heads), F32)
    beta_g = jnp.zeros((BLOCK, heads), F32)
    across = jnp.zeros((heads, BLOCK), F32)
    for j in range(heads // copies):
        cut = slice(j * DK, (j + 1) * DK)
        qn, q_scale = unit_rows(q_ref[0, :, cut].astype(F32))
        khat, k_scale = unit_rows(k_ref[0, :, cut].astype(F32))
        qhat = qn * QSCALE
        qlow, klow = qhat.astype(BF16), khat.astype(BF16)
        pair_k = mm(klow, klow, NT)
        pair_q = mm(qlow, klow, NT)
        qhat_g = jnp.zeros((BLOCK, DK), F32)
        khat_g = jnp.zeros((BLOCK, DK), F32)
        for h in range(j * copies, (j + 1) * copies):
            cut_v = slice(h * DV, (h + 1) * DV)
            decay = decays(cumul, columns, h, strict)
            grow, keep, beta = growth[:, h : h + 1], weight[:, h : h + 1], betas[:, h : h + 1]
            value = v_ref[0, :, cut_v].astype(F32)
            state, back = halves_of(y_ref, h, 0), halves_of(y_ref, h, HALF)
            out_g = hg_ref[:, cut_v]
            decay_in = decay + ident
            scores = pair_q * decay_in
            fresh = (u0_ref[h].astype(F32) - mm(wm_ref[h], state, NT)).astype(BF16)
            fresh_g = mm(scores, out_g, TN) + mm(keep * khat, back, NT)
            rhs_g = mm(t_ref[h], fresh_g, TN)
            rhs_low = rhs_g.astype(BF16)
            read_q = mm(out_g, state)
            read_k = mm(rhs_low, state)
            scores_g = mm(out_g, fresh, NT)
            part_g = jnp.where(strict, -mm(rhs_low, fresh, NT), 0.0) * decay
            pair_qg = (scores_g * decay_in).astype(BF16)
            pair_kg = (part_g * beta).astype(BF16)
            kept_g = mm(fresh, back)
            part_k = part_g * pair_k
            gaps = scores_g * scores + part_k * beta
            low_q = mm(pair_qg, klow).astype(BF16).astype(F32)
            low_k = mm(pair_qg, qlow, TN) + mm(pair_kg, klow) + mm(pair_kg, klow, TN)
            qhat_g += grow * read_q + low_q
            khat_g += keep * kept_g - (beta * grow) * read_k + low_k.astype(BF16).astype(F32)
            dv_ref[0, :, cut_v] = (beta * rhs_g).astype(BF16)
            read_sum = jnp.sum(read_k * khat, axis=1, keepdims=True)
            beta_col = jnp.sum(rhs_g * value + part_k, axis=1, keepdims=True) - grow * read_sum
            kept_sum = jnp.sum(kept_g * khat, axis=1, keepdims=True) * keep
            grow_g = jnp.sum(read_q * qhat, axis=1, keepdims=True) - beta * read_sum
            cumul_col = grow_g * grow + jnp.sum(gaps, axis=1, keepdims=True) - kept_sum
            whole = jnp.sum(back.astype(F32) * state.astype(F32)) * ends[:, h : h + 1]
            at_end = jnp.sum(kept_sum, axis=0, keepdims=True) + whole
            cumul_col += jnp.where(row[:, 0:1] == BLOCK - 1, at_end, 0.0)
            cumul_g = jnp.where(lane == h, cumul_col, cumul_g)
            beta_g = jnp.where(lane == h, beta_col, beta_g)
            across = jnp.where(level == h, jnp.sum(gaps, axis=0, keepdims=True), across)
        q_along = jnp.sum(qn * qhat_g, axis=1, keepdims=True)
        k_along = jnp.sum(khat * khat_g, axis=1, keepdims=True)
        dq_ref[0, :, cut] = ((q_scale * QSCALE) * (qhat_g - qn * q_along)).astype(BF16)
        dk_ref[0, :, cut] = (k_scale * (khat_g - khat * k_along)).astype(BF16)
    db_ref[0] = beta_g.T
    dg_ref[0] = exact(cumul_g.T - across, (row >= col).astype(F32))


def whole(x):
    return pl.BlockSpec(x.shape, lambda *i: (0,) * len(x.shape))


SCALAR = pl.BlockSpec(memory_space=pltpu.SMEM)
HELD = pl.BlockSpec(memory_space=pltpu.VMEM)
FAR = pl.BlockSpec(memory_space=pl.ANY)


def call(kernel, outs, *args, ins=None, out_specs=None, flops=0, scratch=(), grid=(), limit=24, **more):
    size = sum(math.prod(x.shape) * x.dtype.itemsize for x in (*args, *outs))
    return pl.pallas_call(
        kernel,
        grid=grid,
        out_shape=outs,
        in_specs=[HELD] * len(args) if ins is None else ins,
        out_specs=[HELD] * len(outs) if out_specs is None else out_specs,
        scratch_shapes=scratch,
        compiler_params=pltpu.CompilerParams(vmem_limit_bytes=limit * 2**20),
        cost_estimate=pl.CostEstimate(flops=flops, bytes_accessed=size, transcendentals=0),
        **more,
    )(*args)


def shape(dims, dtype):
    return jax.ShapeDtypeStruct(dims, dtype)


def far(dims, dtype):
    return pltpu.HBM(dims, dtype)


def fixed(x):
    return pltpu.with_memory_space_constraint(x, pltpu.HBM)


def body(
    queries, key_rows, value_rows, log_decay, write_rate,
    initial_state, final_state_grad, output_matrix, output_grad,
):
    heads = log_decay.shape[1]
    blocks = lax.axis_size("ctx")
    feats = lax.axis_size("tp")
    here, core = lax.axis_index("ctx"), lax.axis_index("dp")
    rows, wide = output_matrix.shape
    piece = rows // blocks
    swap = [(0, 1), (1, 0)]
    square = (heads, BLOCK, DK)
    unit = 2 * BLOCK**3 * heads

    def own_half(states):
        parts = states.reshape(blocks, HALF, DK)
        return lax.dynamic_index_in_dim(parts, here, 0, keepdims=False)

    with jax.named_scope("gather_grad"):
        grads = [output_grad]
        for k in range(1, feats):
            pairs = [((i + k) % feats, i) for i in range(feats)]
            grads.append(lax.ppermute(output_grad, "tp", pairs))
    with jax.named_scope("other_rows"):
        other_matrix = lax.ppermute(output_matrix, "dp", swap)
    dma = pltpu.SemaphoreType.DMA
    with jax.named_scope("local_maps"):
        args = tuple(map(fixed, (queries, key_rows, value_rows, log_decay, write_rate)))
        outs = [far((blocks, 2 * DK, DK), BF16)] + [far(square, BF16)] * 5
        maps, t, wm, u0, qe, o0 = call(
            local_maps, outs, *args,
            ins=[whole(a) for a in args], out_specs=[whole(o) for o in outs], grid=(1,),
            flops=50 * unit,
        )
    with jax.named_scope("head_grads"):
        maps, head_grad, mine, theirs = call(
            head_grads,
            [far(maps.shape, BF16), shape((BLOCK, wide), BF16)]
            + [shape((BLOCK, rows), BF16)] * 2,
            jnp.stack([core, lax.axis_index("tp")]), *grads,
            fixed(output_matrix), other_matrix, fixed(qe), fixed(maps),
            ins=[SCALAR] + [HELD] * feats + [FAR, HELD, FAR, FAR],
            out_specs=[FAR, HELD, HELD, HELD],
            scratch=[
                pltpu.VMEM((feats,) + output_grad.shape[1:], BF16),
                pltpu.VMEM(output_matrix.shape, BF16),
                pltpu.VMEM(square, BF16),
                pltpu.VMEM((blocks, HALF, DK), BF16),
                dma((2,)),
                dma(()),
            ],
            flops=18 * unit,
            input_output_aliases={feats + 4: 0},
        )
        theirs = lax.ppermute(theirs, "dp", swap)
    with jax.named_scope("send_maps"):
        maps = lax.all_to_all(maps, "ctx", 0, 0, tiled=True)
    with jax.named_scope("chain"):
        states, = call(
            chain, [far((blocks, 2 * HALF, DK), BF16)],
            maps, own_half(initial_state), own_half(final_state_grad),
            out_specs=[FAR],
            scratch=[pltpu.VMEM((blocks, 2 * HALF, DK), BF16), dma((blocks, 2))],
            flops=4 * unit,
        )
    with jax.named_scope("return_states"):
        states = lax.all_to_all(states, "ctx", 0, 0, tiled=True)
    with jax.named_scope("outputs"):
        heads_low, = call(
            outputs, [shape((BLOCK, wide), BF16)], qe, o0, states, flops=unit
        )
        other_low = lax.ppermute(heads_low, "dp", swap)
    with jax.named_scope("projection"):
        pieces = (blocks, piece, wide)
        partial, = call(
            projection, [far(pieces, BF16)], mine, theirs, heads_low, other_low,
            out_specs=[FAR], scratch=[pltpu.VMEM(pieces, BF16), dma((4,))], flops=16 * unit,
        )
        partial = lax.all_to_all(partial, "ctx", 0, 0, tiled=True)
        spread, = call(
            functools.partial(reduce_spread, float(BLOCK * blocks * lax.axis_size("dp")) ** (-0.5)),
            [far(pieces, BF16)], partial,
            out_specs=[FAR], scratch=[pltpu.VMEM((piece, wide), BF16), dma((blocks, 2))],
        )
        total = lax.all_to_all(spread, "ctx", 0, 0, tiled=True).reshape(rows, wide)
        weight_grad, = call(
            widen, [far((rows, wide), F32)], total,
            out_specs=[FAR], scratch=[pltpu.VMEM((rows, wide), F32), dma((8,))],
        )
    with jax.named_scope("gradients"):
        args += (fixed(t), fixed(wm), fixed(u0), head_grad, states)
        outs = [far(x.shape, x.dtype) for x in args[:5]]
        query_g, key_g, value_g, decay_g, rate_g = call(
            gradients, outs, *args,
            ins=[whole(a) for a in args], out_specs=[whole(o) for o in outs], grid=(1,),
            flops=17 * unit,
        )
    return (query_g, key_g, value_g, decay_g, rate_g, weight_grad)


def solution(mesh):
    rows = P("dp", "ctx", "tp")
    gates = P("dp", "tp", "ctx")
    state = P("dp", "tp", None, None)
    return jax.shard_map(
        body,
        mesh=mesh,
        in_specs=(rows, rows, rows, gates, gates, state, state, P("dp", "tp"), rows),
        out_specs=(rows, rows, rows, gates, gates, P("dp", "tp")),
        check_vma=False,
    )
```

```python
import functools
import math

import jax
import jax.numpy as jnp
from jax import lax
from jax.experimental import pallas as pl
from jax.experimental.pallas import tpu as pltpu
from jax.sharding import PartitionSpec as P

DK = 128
DV = 128
BLOCK = 128
HALF = DV // 2
F32 = jnp.float32
BF16 = jnp.bfloat16
QSCALE = DK ** (-0.5)

NN = (((1,), (0,)), ((), ()))
NT = (((1,), (1,)), ((), ()))
TN = (((0,), (0,)), ((), ()))


def mm(a, b, dims=NN):
    return lax.dot_general(a.astype(BF16), b.astype(BF16), dims, preferred_element_type=F32)


def split(a):
    high = a.astype(BF16)
    return high, (a - high.astype(F32)).astype(BF16)


def mm_left(a, b, dims=NN):
    low = b.astype(BF16)
    return mm(a[0], low, dims) + mm(a[1], low, dims)


def mm_right(a, b, dims=NN):
    low = a.astype(BF16)
    return mm(low, b[0], dims) + mm(low, b[1], dims)


def exact(a, b):
    return lax.dot_general(
        a, b, NN, precision=lax.Precision.HIGHEST, preferred_element_type=F32
    )


def iotas():
    row = lax.broadcasted_iota(jnp.int32, (BLOCK, BLOCK), 0)
    col = lax.broadcasted_iota(jnp.int32, (BLOCK, BLOCK), 1)
    return row, col


def unit_rows(rows):
    scale = lax.rsqrt(jnp.sum(rows * rows, axis=-1, keepdims=True) + 1e-06)
    return rows * scale, scale


def gate_columns(gates, row, col):
    cumul = exact(gates, (row <= col).astype(F32))
    columns = cumul.T
    last = columns[BLOCK - 1 : BLOCK, :]
    return cumul, columns, jnp.exp(columns), jnp.exp(last - columns), jnp.exp(last)


def decays(cumul, columns, h, strict):
    gap = columns[:, h : h + 1] - cumul[h : h + 1, :]
    return jnp.where(strict, jnp.exp(jnp.where(strict, gap, 0.0)), 0.0)


def unit_lower_inverses(parts, row, col):
    ident = (row == col).astype(F32)
    found = None
    size = 1
    while size < BLOCK:
        off = (row // (2 * size) == col // (2 * size)) & (row // size != col // size)
        offs = [jnp.where(off, a, 0.0) for a in parts]
        if size == 1:
            found = [ident - a for a in offs]
        else:
            lows = [t.astype(BF16) for t in found]
            inner = [mm(t, a) for t, a in zip(lows, offs)]
            found = [t - mm(x, s) for t, x, s in zip(found, inner, lows)]
        size *= 2
    lows = [t.astype(BF16) for t in found]
    rest = [ident - (t.astype(F32) + mm_left(split(a), t)) for t, a in zip(lows, parts)]
    return [t.astype(F32) + mm(t, r) for t, r in zip(lows, rest)]


class Heads:
    def __init__(self, q_ref, k_ref, g_ref, b_ref):
        self.count = g_ref.shape[1]
        self.copies = self.count * DK // q_ref.shape[2]
        self.row, self.col = iotas()
        self.ident = (self.row == self.col).astype(F32)
        strict = self.row > self.col
        cumul, columns, growth, weight, ends = gate_columns(g_ref[0], self.row, self.col)
        betas = b_ref[0].T
        one = [slice(h, h + 1) for h in range(self.count)]
        self.decay = [decays(cumul, columns, h, strict) for h in range(self.count)]
        self.beta, self.grow, self.keep, self.end = (
            [x[:, cut] for cut in one] for x in (betas, growth, weight, ends)
        )
        self.qn, self.q_scale, self.khat, self.k_scale = [], [], [], []
        self.pair_k, self.pair_q = [], []
        for j in range(self.count // self.copies):
            cut = slice(j * DK, (j + 1) * DK)
            qn, q_scale = unit_rows(q_ref[0, :, cut].astype(F32))
            khat, k_scale = unit_rows(k_ref[0, :, cut].astype(F32))
            self.qn.append(qn)
            self.q_scale.append(q_scale)
            self.khat.append(khat)
            self.k_scale.append(k_scale)
            self.pair_k.append(mm(khat, khat, NT))
            self.pair_q.append(mm(qn * QSCALE, khat, NT))
        parts = [
            self.beta[h] * self.pair_k[h // self.copies] * self.decay[h] for h in range(self.count)
        ]
        self.inverse = [split(t) for t in unit_lower_inverses(parts, self.row, self.col)]


def local_maps(q_ref, k_ref, v_ref, g_ref, b_ref, pay_ref, qe_ref, o0_ref):
    x = Heads(q_ref, k_ref, g_ref, b_ref)
    for h in range(x.count):
        j = h // x.copies
        value = v_ref[0, :, h * DV : (h + 1) * DV].astype(F32)
        wm = mm_left(x.inverse[h], (x.beta[h] * x.grow[h]) * x.khat[j])
        u0 = mm_left(x.inverse[h], x.beta[h] * value)
        kw = split(x.keep[h] * x.khat[j])
        step = (x.end[h] * x.ident - mm_right(wm, kw, TN)).astype(BF16)
        write = mm_right(u0, kw, TN).astype(BF16)
        scores = x.pair_q[j] * (x.decay[h] + x.ident)
        qe_ref[h] = (x.grow[h] * (x.qn[j] * QSCALE) - mm(scores, wm)).astype(BF16)
        o0_ref[h] = mm(scores, u0).astype(BF16)
        for half in range(2):
            pay_ref[2 * h + half, 0:DK] = step
            pay_ref[2 * h + half, DK : DK + HALF] = write[half * HALF : (half + 1) * HALF]


def head_grads(
    at_ref, g0_ref, g1_ref, g2_ref, g3_ref, own_hbm, other_ref, qe_hbm, pay_in,
    pay_ref, hg_ref, mine_ref, theirs_ref, all_ref, own_ref, qe_ref, back_ref, in_sems, out_sem,
):
    fetch = pltpu.make_async_copy(own_hbm, own_ref, in_sems.at[0])
    fetch_qe = pltpu.make_async_copy(qe_hbm, qe_ref, in_sems.at[1])
    fetch.start()
    fetch_qe.start()
    core, here = at_ref[0], at_ref[1]
    feats, wide = all_ref.shape[0], all_ref.shape[2]
    parts = feats // 2
    for k, ref in enumerate((g0_ref, g1_ref, g2_ref, g3_ref)):
        all_ref[lax.rem(here + k, feats)] = ref[0]
    total = jnp.zeros((BLOCK, own_ref.shape[1]), F32)
    for i in range(parts):
        cut = slice(i * wide, (i + 1) * wide)
        theirs = all_ref[parts * (1 - core) + i]
        total += mm(theirs, other_ref[cut, :])
        theirs_ref[:, cut] = theirs
    fetch.wait()
    for i in range(parts):
        cut = slice(i * wide, (i + 1) * wide)
        mine = all_ref[parts * core + i]
        total += mm(mine, own_ref[cut, :])
        mine_ref[:, cut] = mine
    total = total.astype(BF16)
    hg_ref[...] = total
    fetch_qe.wait()
    for h in range(qe_ref.shape[0]):
        back = mm(total[:, h * DV : (h + 1) * DV], qe_ref[h], TN).astype(BF16)
        for half in range(2):
            back_ref[2 * h + half] = back[half * HALF : (half + 1) * HALF]
    put = pltpu.make_async_copy(back_ref, pay_ref.at[:, pl.ds(DK + HALF, HALF)], out_sem)
    put.start()
    put.wait()


def chain(maps_ref, first_ref, last_ref, out_ref, kept_ref, sems):
    blocks = maps_ref.shape[0]
    copies = []

    def times(state, step, dims):
        out = mm(jnp.concatenate(split(state), axis=0), step, dims)
        return out[:HALF] + out[HALF:]

    def send(value, c, side):
        rows = pl.ds(side * HALF, HALF)
        kept_ref[c, rows] = value.astype(BF16)
        copy = pltpu.make_async_copy(kept_ref.at[c, rows], out_ref.at[c, rows], sems.at[c, side])
        copy.start()
        copies.append(copy)

    state, back = first_ref[...], last_ref[...]
    for c in range(blocks):
        e = blocks - 1 - c
        send(state, c, 0)
        send(back, e, 1)
        if c < blocks - 1:
            write = maps_ref[c, DK : DK + HALF].astype(F32)
            read = maps_ref[e, DK + HALF :].astype(F32)
            state = times(state, maps_ref[c, 0:DK], NN) + write
            back = times(back, maps_ref[e, 0:DK], NT) + read
    for copy in copies:
        copy.wait()


def projection(mine_ref, theirs_ref, low_ref, other_ref, out_ref, kept_ref, sems):
    blocks, piece = out_ref.shape[0], out_ref.shape[1]
    parts = sems.shape[0]
    some = blocks // parts
    copies = []
    for p in range(parts):
        cut = slice(p * some * piece, (p + 1) * some * piece)
        total = mm(mine_ref[:, cut], low_ref[...], TN) + mm(theirs_ref[:, cut], other_ref[...], TN)
        total = total.astype(BF16)
        for c in range(some):
            kept_ref[p * some + c] = total[c * piece : (c + 1) * piece]
        at = pl.ds(p * some, some)
        copies.append(pltpu.make_async_copy(kept_ref.at[at], out_ref.at[at], sems.at[p]))
        copies[-1].start()
    for copy in copies:
        copy.wait()


def reduce_spread(scale, pieces_ref, out_ref, sum_ref, sems):
    blocks, rows = out_ref.shape[:2]
    parts = sems.shape[1]
    copies = []
    for p in range(parts):
        at = pl.ds(p * (rows // parts), rows // parts)
        total = pieces_ref[0, at].astype(F32)
        for c in range(1, blocks):
            total += pieces_ref[c, at].astype(F32)
        sum_ref[at] = (total * scale).astype(BF16)
        for c in range(blocks):
            copy = pltpu.make_async_copy(sum_ref.at[at], out_ref.at[c, at], sems.at[c, p])
            copy.start()
            copies.append(copy)
    for copy in copies:
        copy.wait()


def widen(in_ref, out_ref, kept_ref, sems):
    parts = sems.shape[0]
    step = in_ref.shape[0] // parts
    copies = []
    for p in range(parts):
        at = pl.ds(p * step, step)
        kept_ref[at, :] = in_ref[at, :].astype(F32)
        copies.append(pltpu.make_async_copy(kept_ref.at[at], out_ref.at[at], sems.at[p]))
        copies[-1].start()
    for copy in copies:
        copy.wait()


def halves_of(ref, h, low):
    rows = slice(low, low + HALF)
    return jnp.concatenate([ref[2 * h, rows], ref[2 * h + 1, rows]], axis=0)


def outputs(qe_ref, o0_ref, y_ref, o_ref):
    for h in range(qe_ref.shape[0]):
        out = o0_ref[h].astype(F32) + mm(qe_ref[h], halves_of(y_ref, h, 0), NT)
        o_ref[:, h * DV : (h + 1) * DV] = out.astype(BF16)


def gradients(
    q_ref, k_ref, v_ref, g_ref, b_ref, hg_ref, y_ref,
    dq_ref, dk_ref, dv_ref, dg_ref, db_ref,
):
    x = Heads(q_ref, k_ref, g_ref, b_ref)
    row, col = x.row, x.col
    strict = row > col
    lane = lax.broadcasted_iota(jnp.int32, (BLOCK, x.count), 1)
    level = lax.broadcasted_iota(jnp.int32, (x.count, BLOCK), 0)
    cumul_g = jnp.zeros((BLOCK, x.count), F32)
    beta_g = jnp.zeros((BLOCK, x.count), F32)
    across = jnp.zeros((x.count, BLOCK), F32)
    for j in range(x.count // x.copies):
        cut = slice(j * DK, (j + 1) * DK)
        qn, khat = x.qn[j], x.khat[j]
        qhat = qn * QSCALE
        qlow, klow = qhat.astype(BF16), khat.astype(BF16)
        pair_k, pair_q = x.pair_k[j], x.pair_q[j]
        qhat_g = jnp.zeros((BLOCK, DK), F32)
        khat_g = jnp.zeros((BLOCK, DK), F32)
        for h in range(j * x.copies, (j + 1) * x.copies):
            cut_v = slice(h * DV, (h + 1) * DV)
            decay, grow, keep, beta = x.decay[h], x.grow[h], x.keep[h], x.beta[h]
            value = v_ref[0, :, cut_v].astype(F32)
            state, back = halves_of(y_ref, h, 0), halves_of(y_ref, h, HALF)
            out_g = hg_ref[:, cut_v]
            decay_in = decay + x.ident
            scores = pair_q * decay_in
            fresh = mm_left(x.inverse[h], beta * (value - grow * mm(klow, state, NT))).astype(BF16)
            fresh_g = mm(scores, out_g, TN) + mm(keep * khat, back, NT)
            rhs_g = mm(x.inverse[h][0], fresh_g, TN)
            rhs_low = rhs_g.astype(BF16)
            read_q = mm(out_g, state)
            read_k = mm(rhs_low, state)
            scores_g = mm(out_g, fresh, NT)
            part_g = jnp.where(strict, -mm(rhs_low, fresh, NT), 0.0) * decay
            pair_qg = (scores_g * decay_in).astype(BF16)
            pair_kg = (part_g * beta).astype(BF16)
            kept_g = mm(fresh, back)
            part_k = part_g * pair_k
            gaps = scores_g * scores + part_k * beta
            low_q = mm(pair_qg, klow).astype(BF16).astype(F32)
            low_k = mm(pair_qg, qlow, TN) + mm(pair_kg, klow) + mm(pair_kg, klow, TN)
            qhat_g += grow * read_q + low_q
            khat_g += keep * kept_g - (beta * grow) * read_k + low_k.astype(BF16).astype(F32)
            dv_ref[0, :, cut_v] = (beta * rhs_g).astype(BF16)
            read_sum = jnp.sum(read_k * khat, axis=1, keepdims=True)
            beta_col = jnp.sum(rhs_g * value + part_k, axis=1, keepdims=True) - grow * read_sum
            kept_sum = jnp.sum(kept_g * khat, axis=1, keepdims=True) * keep
            grow_g = jnp.sum(read_q * qhat, axis=1, keepdims=True) - beta * read_sum
            cumul_col = grow_g * grow + jnp.sum(gaps, axis=1, keepdims=True) - kept_sum
            whole = jnp.sum(back.astype(F32) * state.astype(F32)) * x.end[h]
            at_end = jnp.sum(kept_sum, axis=0, keepdims=True) + whole
            cumul_col += jnp.where(row[:, 0:1] == BLOCK - 1, at_end, 0.0)
            cumul_g = jnp.where(lane == h, cumul_col, cumul_g)
            beta_g = jnp.where(lane == h, beta_col, beta_g)
            across = jnp.where(level == h, jnp.sum(gaps, axis=0, keepdims=True), across)
        q_along = jnp.sum(qn * qhat_g, axis=1, keepdims=True)
        k_along = jnp.sum(khat * khat_g, axis=1, keepdims=True)
        dq_ref[0, :, cut] = ((x.q_scale[j] * QSCALE) * (qhat_g - qn * q_along)).astype(BF16)
        dk_ref[0, :, cut] = (x.k_scale[j] * (khat_g - khat * k_along)).astype(BF16)
    db_ref[0] = beta_g.T
    dg_ref[0] = exact(cumul_g.T - across, (row >= col).astype(F32))


def gradients_on(turn, at_ref, *refs):
    *held, sems = refs[-13:]
    far_in = refs[:7]
    far_out = refs[7 + (1 if turn else 6) :][:5]

    @pl.when(at_ref[0] == turn)
    def _():
        fetches = [pltpu.make_async_copy(far_in[i], held[i], sems.at[i]) for i in range(7)]
        for copy in fetches:
            copy.start()
        for copy in fetches:
            copy.wait()
        gradients(*held)
        puts = [pltpu.make_async_copy(held[7 + i], far_out[i], sems.at[7 + i]) for i in range(5)]
        for copy in puts:
            copy.start()
        for copy in puts:
            copy.wait()


def whole(x):
    return pl.BlockSpec(x.shape, lambda *i: (0,) * len(x.shape))


SCALAR = pl.BlockSpec(memory_space=pltpu.SMEM)
HELD = pl.BlockSpec(memory_space=pltpu.VMEM)
FAR = pl.BlockSpec(memory_space=pl.ANY)


def call(kernel, outs, *args, ins=None, out_specs=None, flops=0, scratch=(), grid=(), limit=24, **more):
    size = sum(math.prod(x.shape) * x.dtype.itemsize for x in (*args, *outs))
    return pl.pallas_call(
        kernel,
        grid=grid,
        out_shape=outs,
        in_specs=[HELD] * len(args) if ins is None else ins,
        out_specs=[HELD] * len(outs) if out_specs is None else out_specs,
        scratch_shapes=scratch,
        compiler_params=pltpu.CompilerParams(vmem_limit_bytes=limit * 2**20),
        cost_estimate=pl.CostEstimate(flops=flops, bytes_accessed=size, transcendentals=0),
        **more,
    )(*args)


def shape(dims, dtype):
    return jax.ShapeDtypeStruct(dims, dtype)


def far(dims, dtype):
    return pltpu.HBM(dims, dtype)


def fixed(x):
    return pltpu.with_memory_space_constraint(x, pltpu.HBM)


def body(
    queries, key_rows, value_rows, log_decay, write_rate,
    initial_state, final_state_grad, output_matrix, output_grad,
):
    heads = log_decay.shape[1]
    blocks = lax.axis_size("ctx")
    feats = lax.axis_size("tp")
    here, core = lax.axis_index("ctx"), lax.axis_index("dp")
    rows, wide = output_matrix.shape
    piece = rows // blocks
    swap = [(0, 1), (1, 0)]
    square = (heads, BLOCK, DK)
    unit = 2 * BLOCK**3 * heads

    def own_half(states):
        parts = states.reshape(blocks, HALF, DK)
        return lax.dynamic_index_in_dim(parts, here, 0, keepdims=False)

    with jax.named_scope("gather_grad"):
        grads = [output_grad]
        for k in range(1, feats):
            pairs = [((i + k) % feats, i) for i in range(feats)]
            grads.append(lax.ppermute(output_grad, "tp", pairs))
    with jax.named_scope("other_rows"):
        other_matrix = lax.ppermute(output_matrix, "dp", swap)
    dma = pltpu.SemaphoreType.DMA
    with jax.named_scope("local_maps"):
        args = tuple(map(fixed, (queries, key_rows, value_rows, log_decay, write_rate)))
        outs = [far((blocks, 2 * DK, DK), BF16)] + [far(square, BF16)] * 2
        maps, qe, o0 = call(
            local_maps, outs, *args,
            ins=[whole(a) for a in args], out_specs=[whole(o) for o in outs], grid=(1,),
            flops=50 * unit,
        )
    with jax.named_scope("head_grads"):
        maps, head_grad, mine, theirs = call(
            head_grads,
            [far(maps.shape, BF16), shape((BLOCK, wide), BF16)]
            + [shape((BLOCK, rows), BF16)] * 2,
            jnp.stack([core, lax.axis_index("tp")]), *grads,
            fixed(output_matrix), other_matrix, fixed(qe), fixed(maps),
            ins=[SCALAR] + [HELD] * feats + [FAR, HELD, FAR, FAR],
            out_specs=[FAR, HELD, HELD, HELD],
            scratch=[
                pltpu.VMEM((feats,) + output_grad.shape[1:], BF16),
                pltpu.VMEM(output_matrix.shape, BF16),
                pltpu.VMEM(square, BF16),
                pltpu.VMEM((blocks, HALF, DK), BF16),
                dma((2,)),
                dma(()),
            ],
            flops=18 * unit,
            input_output_aliases={feats + 4: 0},
        )
        theirs = lax.ppermute(theirs, "dp", swap)
    with jax.named_scope("send_maps"):
        maps = lax.all_to_all(maps, "ctx", 0, 0, tiled=True)
    with jax.named_scope("chain"):
        states, = call(
            chain, [far((blocks, 2 * HALF, DK), BF16)],
            maps, own_half(initial_state), own_half(final_state_grad),
            out_specs=[FAR],
            scratch=[pltpu.VMEM((blocks, 2 * HALF, DK), BF16), dma((blocks, 2))],
            flops=4 * unit,
        )
    with jax.named_scope("return_states"):
        states = lax.all_to_all(states, "ctx", 0, 0, tiled=True)
    with jax.named_scope("outputs"):
        heads_low, = call(
            outputs, [shape((BLOCK, wide), BF16)], qe, o0, states, flops=unit
        )
        other_low = lax.ppermute(heads_low, "dp", swap)
    with jax.named_scope("projection"):
        pieces = (blocks, piece, wide)
        partial, = call(
            projection, [far(pieces, BF16)], mine, theirs, heads_low, other_low,
            out_specs=[FAR], scratch=[pltpu.VMEM(pieces, BF16), dma((4,))], flops=16 * unit,
        )
    with jax.named_scope("gradients"):
        args += (head_grad, states)
        outs = [far(x.shape, x.dtype) for x in args[:5]]
        held = [pltpu.VMEM(x.shape, x.dtype) for x in args + args[:5]] + [dma((12,))]
        *found, partial = call(
            functools.partial(gradients_on, 1), outs + [far(pieces, BF16)],
            core.reshape(1), *args, fixed(partial),
            ins=[SCALAR] + [FAR] * 8, out_specs=[FAR] * 6, scratch=held, flops=35 * unit,
            input_output_aliases={8: 5},
        )
    with jax.named_scope("projection"):
        partial = lax.all_to_all(partial, "ctx", 0, 0, tiled=True)
        spread, = call(
            functools.partial(reduce_spread, float(BLOCK * blocks * lax.axis_size("dp")) ** (-0.5)),
            [far(pieces, BF16)], partial,
            out_specs=[FAR], scratch=[pltpu.VMEM((piece, wide), BF16), dma((blocks, 2))],
        )
        total = lax.all_to_all(spread, "ctx", 0, 0, tiled=True).reshape(rows, wide)
        weight_grad, = call(
            widen, [far((rows, wide), F32)], total,
            out_specs=[FAR], scratch=[pltpu.VMEM((rows, wide), F32), dma((8,))],
        )
    with jax.named_scope("gradients"):
        query_g, key_g, value_g, decay_g, rate_g = call(
            functools.partial(gradients_on, 0), outs,
            core.reshape(1), *args, fixed(spread), *map(fixed, found),
            ins=[SCALAR] + [FAR] * 13, out_specs=[FAR] * 5, scratch=held, flops=35 * unit,
            input_output_aliases={9 + i: i for i in range(5)},
        )
    return (query_g, key_g, value_g, decay_g, rate_g, weight_grad)


def solution(mesh):
    rows = P("dp", "ctx", "tp")
    gates = P("dp", "tp", "ctx")
    state = P("dp", "tp", None, None)
    return jax.shard_map(
        body,
        mesh=mesh,
        in_specs=(rows, rows, rows, gates, gates, state, state, P("dp", "tp"), rows),
        out_specs=(rows, rows, rows, gates, gates, P("dp", "tp")),
        check_vma=False,
    )
```

```python
import functools
import math

import jax
import jax.numpy as jnp
from jax import lax
from jax.experimental import pallas as pl
from jax.experimental.pallas import tpu as pltpu
from jax.sharding import PartitionSpec as P

DK = 128
DV = 128
BLOCK = 128
HALF = DV // 2
F32 = jnp.float32
BF16 = jnp.bfloat16
QSCALE = DK ** (-0.5)

NN = (((1,), (0,)), ((), ()))
NT = (((1,), (1,)), ((), ()))
TN = (((0,), (0,)), ((), ()))


def mm(a, b, dims=NN):
    return lax.dot_general(a.astype(BF16), b.astype(BF16), dims, preferred_element_type=F32)


def split(a):
    high = a.astype(BF16)
    return high, (a - high.astype(F32)).astype(BF16)


def mm3(a, b, dims=NN):
    return mm(a[0], b[0], dims) + (mm(a[0], b[1], dims) + mm(a[1], b[0], dims))


def mm_left(a, b, dims=NN):
    low = b.astype(BF16)
    return mm(a[0], low, dims) + mm(a[1], low, dims)


def mm_right(a, b, dims=NN):
    low = a.astype(BF16)
    return mm(low, b[0], dims) + mm(low, b[1], dims)


def exact(a, b):
    return lax.dot_general(
        a, b, NN, precision=lax.Precision.HIGHEST, preferred_element_type=F32
    )


def iotas():
    row = lax.broadcasted_iota(jnp.int32, (BLOCK, BLOCK), 0)
    col = lax.broadcasted_iota(jnp.int32, (BLOCK, BLOCK), 1)
    return row, col


def unit_rows(rows):
    scale = lax.rsqrt(jnp.sum(rows * rows, axis=-1, keepdims=True) + 1e-06)
    return rows * scale, scale


def gate_columns(gates, row, col):
    cumul = exact(gates, (row <= col).astype(F32))
    columns = cumul.T
    last = columns[BLOCK - 1 : BLOCK, :]
    return cumul, columns, jnp.exp(columns), jnp.exp(last - columns), jnp.exp(last)


def decays(cumul, columns, h, strict):
    gap = columns[:, h : h + 1] - cumul[h : h + 1, :]
    return jnp.where(strict, jnp.exp(jnp.where(strict, gap, 0.0)), 0.0)


def unit_lower_inverses(parts, row, col):
    ident = (row == col).astype(F32)
    found = None
    size = 1
    while size < BLOCK:
        off = (row // (2 * size) == col // (2 * size)) & (row // size != col // size)
        offs = [jnp.where(off, a, 0.0) for a in parts]
        if size == 1:
            found = [ident - a for a in offs]
        else:
            lows = [t.astype(BF16) for t in found]
            inner = [mm(t, a) for t, a in zip(lows, offs)]
            found = [t - mm(x, s) for t, x, s in zip(found, inner, lows)]
        size *= 2
    lows = [t.astype(BF16) for t in found]
    rest = [ident - (t.astype(F32) + mm_left(split(a), t)) for t, a in zip(lows, parts)]
    return [t.astype(F32) + mm(t, r) for t, r in zip(lows, rest)]


class Heads:
    def __init__(self, q_ref, k_ref, g_ref, b_ref):
        self.count = g_ref.shape[1]
        self.copies = self.count * DK // q_ref.shape[2]
        self.row, self.col = iotas()
        self.ident = (self.row == self.col).astype(F32)
        strict = self.row > self.col
        cumul, columns, growth, weight, ends = gate_columns(g_ref[0], self.row, self.col)
        betas = b_ref[0].T
        one = [slice(h, h + 1) for h in range(self.count)]
        self.decay = [decays(cumul, columns, h, strict) for h in range(self.count)]
        self.beta, self.grow, self.keep, self.end = (
            [x[:, cut] for cut in one] for x in (betas, growth, weight, ends)
        )
        self.qn, self.q_scale, self.khat, self.k_scale = [], [], [], []
        self.pair_k, self.pair_q = [], []
        for j in range(self.count // self.copies):
            cut = slice(j * DK, (j + 1) * DK)
            qn, q_scale = unit_rows(q_ref[0, :, cut].astype(F32))
            khat, k_scale = unit_rows(k_ref[0, :, cut].astype(F32))
            self.qn.append(qn)
            self.q_scale.append(q_scale)
            self.khat.append(khat)
            self.k_scale.append(k_scale)
            self.pair_k.append(mm(khat, khat, NT))
            self.pair_q.append(mm(qn * QSCALE, khat, NT))
        parts = [
            self.beta[h] * self.pair_k[h // self.copies] * self.decay[h] for h in range(self.count)
        ]
        self.inverse = [split(t) for t in unit_lower_inverses(parts, self.row, self.col)]


def local_maps(q_ref, k_ref, v_ref, g_ref, b_ref, pay_ref, qe_ref, o0_ref):
    x = Heads(q_ref, k_ref, g_ref, b_ref)
    for h in range(x.count):
        j = h // x.copies
        value = v_ref[0, :, h * DV : (h + 1) * DV].astype(F32)
        wm = mm_left(x.inverse[h], (x.beta[h] * x.grow[h]) * x.khat[j])
        u0 = mm_left(x.inverse[h], x.beta[h] * value)
        kw = split(x.keep[h] * x.khat[j])
        step = (x.end[h] * x.ident - mm_right(wm, kw, TN)).astype(BF16)
        write = mm_right(u0, kw, TN).astype(BF16)
        scores = x.pair_q[j] * (x.decay[h] + x.ident)
        qe_ref[h] = (x.grow[h] * (x.qn[j] * QSCALE) - mm(scores, wm)).astype(BF16)
        o0_ref[h] = mm(scores, u0).astype(BF16)
        for half in range(2):
            pay_ref[2 * h + half, 0:DK] = step
            pay_ref[2 * h + half, DK : DK + HALF] = write[half * HALF : (half + 1) * HALF]


def head_grads(
    at_ref, g0_ref, g1_ref, g2_ref, g3_ref, own_hbm, other_ref, qe_hbm, pay_in,
    pay_ref, hg_ref, mine_ref, theirs_ref, all_ref, own_ref, qe_ref, back_ref, in_sems, out_sems,
):
    fetch = pltpu.make_async_copy(own_hbm, own_ref, in_sems.at[0])
    fetch_qe = pltpu.make_async_copy(qe_hbm, qe_ref, in_sems.at[1])
    fetch.start()
    fetch_qe.start()
    core, here = at_ref[0], at_ref[1]
    feats, wide = all_ref.shape[0], all_ref.shape[2]
    parts = feats // 2
    for k, ref in enumerate((g0_ref, g1_ref, g2_ref, g3_ref)):
        all_ref[lax.rem(here + k, feats)] = ref[0]
    total = jnp.zeros((BLOCK, own_ref.shape[1]), F32)
    for i in range(parts):
        cut = slice(i * wide, (i + 1) * wide)
        theirs = all_ref[parts * (1 - core) + i]
        total += mm(theirs, other_ref[cut, :])
        theirs_ref[:, cut] = theirs
    fetch.wait()
    for i in range(parts):
        cut = slice(i * wide, (i + 1) * wide)
        mine = all_ref[parts * core + i]
        total += mm(mine, own_ref[cut, :])
        mine_ref[:, cut] = mine
    total = total.astype(BF16)
    hg_ref[...] = total
    fetch_qe.wait()
    parts = out_sems.shape[0]
    some = qe_ref.shape[0] // parts
    puts = []
    for p in range(parts):
        for h in range(p * some, (p + 1) * some):
            back = mm(total[:, h * DV : (h + 1) * DV], qe_ref[h], TN).astype(BF16)
            for half in range(2):
                back_ref[2 * h + half] = back[half * HALF : (half + 1) * HALF]
        at = pl.ds(2 * p * some, 2 * some)
        out = pay_ref.at[at, pl.ds(DK + HALF, HALF)]
        puts.append(pltpu.make_async_copy(back_ref.at[at], out, out_sems.at[p]))
        puts[-1].start()
    for copy in puts:
        copy.wait()


def chain(maps_ref, first_ref, last_ref, out_ref, kept_ref, sems):
    blocks = maps_ref.shape[0]
    copies = []

    def times(state, step, dims):
        out = mm(jnp.concatenate(split(state), axis=0), step, dims)
        return out[:HALF] + out[HALF:]

    def send(value, c, side):
        rows = pl.ds(side * HALF, HALF)
        kept_ref[c, rows] = value.astype(BF16)
        copy = pltpu.make_async_copy(kept_ref.at[c, rows], out_ref.at[c, rows], sems.at[c, side])
        copy.start()
        copies.append(copy)

    state, back = first_ref[...], last_ref[...]
    for c in range(blocks):
        e = blocks - 1 - c
        send(state, c, 0)
        send(back, e, 1)
        if c < blocks - 1:
            write = maps_ref[c, DK : DK + HALF].astype(F32)
            read = maps_ref[e, DK + HALF :].astype(F32)
            state = times(state, maps_ref[c, 0:DK], NN) + write
            back = times(back, maps_ref[e, 0:DK], NT) + read
    for copy in copies:
        copy.wait()


def projection(mine_ref, theirs_ref, low_ref, other_ref, out_ref, kept_ref, sems):
    blocks, piece = out_ref.shape[0], out_ref.shape[1]
    parts = sems.shape[0]
    some = blocks // parts
    copies = []
    for p in range(parts):
        cut = slice(p * some * piece, (p + 1) * some * piece)
        total = mm(mine_ref[:, cut], low_ref[...], TN) + mm(theirs_ref[:, cut], other_ref[...], TN)
        total = total.astype(BF16)
        for c in range(some):
            kept_ref[p * some + c] = total[c * piece : (c + 1) * piece]
        at = pl.ds(p * some, some)
        copies.append(pltpu.make_async_copy(kept_ref.at[at], out_ref.at[at], sems.at[p]))
        copies[-1].start()
    for copy in copies:
        copy.wait()


def reduce_spread(scale, pieces_ref, out_ref, sum_ref, sems):
    blocks, rows = out_ref.shape[:2]
    parts = sems.shape[1]
    copies = []
    for p in range(parts):
        at = pl.ds(p * (rows // parts), rows // parts)
        total = pieces_ref[0, at].astype(F32)
        for c in range(1, blocks):
            total += pieces_ref[c, at].astype(F32)
        sum_ref[at] = (total * scale).astype(BF16)
        for c in range(blocks):
            copy = pltpu.make_async_copy(sum_ref.at[at], out_ref.at[c, at], sems.at[c, p])
            copy.start()
            copies.append(copy)
    for copy in copies:
        copy.wait()


def widen(in_ref, out_ref, kept_ref, sems):
    parts = sems.shape[0]
    step = in_ref.shape[0] // parts
    copies = []
    for p in range(parts):
        at = pl.ds(p * step, step)
        kept_ref[at, :] = in_ref[at, :].astype(F32)
        copies.append(pltpu.make_async_copy(kept_ref.at[at], out_ref.at[at], sems.at[p]))
        copies[-1].start()
    for copy in copies:
        copy.wait()


def halves_of(ref, h, low):
    rows = slice(low, low + HALF)
    return jnp.concatenate([ref[2 * h, rows], ref[2 * h + 1, rows]], axis=0)


def outputs(qe_ref, o0_ref, y_ref, o_ref):
    for h in range(qe_ref.shape[0]):
        out = o0_ref[h].astype(F32) + mm(qe_ref[h], halves_of(y_ref, h, 0), NT)
        o_ref[:, h * DV : (h + 1) * DV] = out.astype(BF16)


def gradients(
    q_ref, k_ref, v_ref, g_ref, b_ref, hg_ref, y_ref,
    dq_ref, dk_ref, dv_ref, dg_ref, db_ref,
):
    x = Heads(q_ref, k_ref, g_ref, b_ref)
    row, col = x.row, x.col
    strict = row > col
    lane = lax.broadcasted_iota(jnp.int32, (BLOCK, x.count), 1)
    level = lax.broadcasted_iota(jnp.int32, (x.count, BLOCK), 0)
    cumul_g = jnp.zeros((BLOCK, x.count), F32)
    beta_g = jnp.zeros((BLOCK, x.count), F32)
    across = jnp.zeros((x.count, BLOCK), F32)
    for j in range(x.count // x.copies):
        cut = slice(j * DK, (j + 1) * DK)
        qn, khat = x.qn[j], x.khat[j]
        qhat = qn * QSCALE
        qlow, klow = qhat.astype(BF16), khat.astype(BF16)
        pair_k, pair_q = x.pair_k[j], x.pair_q[j]
        qhat_g = jnp.zeros((BLOCK, DK), F32)
        khat_g = jnp.zeros((BLOCK, DK), F32)
        for h in range(j * x.copies, (j + 1) * x.copies):
            cut_v = slice(h * DV, (h + 1) * DV)
            decay, grow, keep, beta = x.decay[h], x.grow[h], x.keep[h], x.beta[h]
            value = v_ref[0, :, cut_v].astype(F32)
            state, back = halves_of(y_ref, h, 0), halves_of(y_ref, h, HALF)
            out_g = hg_ref[:, cut_v]
            decay_in = decay + x.ident
            scores = pair_q * decay_in
            inverse = x.inverse[h]
            known = beta * (value - grow * mm_left(split(khat), state, NT))
            fresh = split(mm3(inverse, split(known)))
            fresh_g = mm_left(split(scores), out_g, TN) + mm_left(split(keep * khat), back, NT)
            rhs_g = mm3(inverse, split(fresh_g), TN)
            rhs = split(rhs_g)
            read_q = mm(out_g, state)
            read_k = mm_left(rhs, state)
            scores_g = mm_right(out_g, fresh, NT)
            part_g = jnp.where(strict, -mm3(rhs, fresh, NT), 0.0) * decay
            pair_qg, pair_kg = split(scores_g * decay_in), split(part_g * beta)
            kept_g = mm_left(fresh, back)
            part_k = part_g * pair_k
            gaps = scores_g * scores + part_k * beta
            low_q = mm_left(pair_qg, klow).astype(BF16).astype(F32)
            low_k = mm_left(pair_qg, qlow, TN) + mm_left(pair_kg, klow)
            low_k += mm_left(pair_kg, klow, TN)
            qhat_g += grow * read_q + low_q
            khat_g += keep * kept_g - (beta * grow) * read_k + low_k.astype(BF16).astype(F32)
            dv_ref[0, :, cut_v] = (beta * rhs_g).astype(BF16)
            read_sum = jnp.sum(read_k * khat, axis=1, keepdims=True)
            beta_col = jnp.sum(rhs_g * value + part_k, axis=1, keepdims=True) - grow * read_sum
            kept_sum = jnp.sum(kept_g * khat, axis=1, keepdims=True) * keep
            grow_g = jnp.sum(read_q * qhat, axis=1, keepdims=True) - beta * read_sum
            cumul_col = grow_g * grow + jnp.sum(gaps, axis=1, keepdims=True) - kept_sum
            whole = jnp.sum(back.astype(F32) * state.astype(F32)) * x.end[h]
            at_end = jnp.sum(kept_sum, axis=0, keepdims=True) + whole
            cumul_col += jnp.where(row[:, 0:1] == BLOCK - 1, at_end, 0.0)
            cumul_g = jnp.where(lane == h, cumul_col, cumul_g)
            beta_g = jnp.where(lane == h, beta_col, beta_g)
            across = jnp.where(level == h, jnp.sum(gaps, axis=0, keepdims=True), across)
        q_along = jnp.sum(qn * qhat_g, axis=1, keepdims=True)
        k_along = jnp.sum(khat * khat_g, axis=1, keepdims=True)
        dq_ref[0, :, cut] = ((x.q_scale[j] * QSCALE) * (qhat_g - qn * q_along)).astype(BF16)
        dk_ref[0, :, cut] = (x.k_scale[j] * (khat_g - khat * k_along)).astype(BF16)
    db_ref[0] = beta_g.T
    dg_ref[0] = exact(cumul_g.T - across, (row >= col).astype(F32))


def gradients_on(turn, at_ref, *refs):
    *held, sems = refs[-13:]
    far_in = refs[:7]
    far_out = refs[7 + (1 if turn else 6) :][:5]

    @pl.when(at_ref[0] == turn)
    def _():
        fetches = [pltpu.make_async_copy(far_in[i], held[i], sems.at[i]) for i in range(7)]
        for copy in fetches:
            copy.start()
        for copy in fetches:
            copy.wait()
        gradients(*held)
        puts = [pltpu.make_async_copy(held[7 + i], far_out[i], sems.at[7 + i]) for i in range(5)]
        for copy in puts:
            copy.start()
        for copy in puts:
            copy.wait()


def whole(x):
    return pl.BlockSpec(x.shape, lambda *i: (0,) * len(x.shape))


SCALAR = pl.BlockSpec(memory_space=pltpu.SMEM)
HELD = pl.BlockSpec(memory_space=pltpu.VMEM)
FAR = pl.BlockSpec(memory_space=pl.ANY)


def call(kernel, outs, *args, ins=None, out_specs=None, flops=0, scratch=(), grid=(), limit=24, **more):
    size = sum(math.prod(x.shape) * x.dtype.itemsize for x in (*args, *outs))
    return pl.pallas_call(
        kernel,
        grid=grid,
        out_shape=outs,
        in_specs=[HELD] * len(args) if ins is None else ins,
        out_specs=[HELD] * len(outs) if out_specs is None else out_specs,
        scratch_shapes=scratch,
        compiler_params=pltpu.CompilerParams(vmem_limit_bytes=limit * 2**20),
        cost_estimate=pl.CostEstimate(flops=flops, bytes_accessed=size, transcendentals=0),
        **more,
    )(*args)


def shape(dims, dtype):
    return jax.ShapeDtypeStruct(dims, dtype)


def far(dims, dtype):
    return pltpu.HBM(dims, dtype)


def fixed(x):
    return pltpu.with_memory_space_constraint(x, pltpu.HBM)


def body(
    queries, key_rows, value_rows, log_decay, write_rate,
    initial_state, final_state_grad, output_matrix, output_grad,
):
    heads = log_decay.shape[1]
    blocks = lax.axis_size("ctx")
    feats = lax.axis_size("tp")
    here, core = lax.axis_index("ctx"), lax.axis_index("dp")
    rows, wide = output_matrix.shape
    piece = rows // blocks
    swap = [(0, 1), (1, 0)]
    square = (heads, BLOCK, DK)
    unit = 2 * BLOCK**3 * heads

    def own_half(states):
        parts = states.reshape(blocks, HALF, DK)
        return lax.dynamic_index_in_dim(parts, here, 0, keepdims=False)

    with jax.named_scope("gather_grad"):
        grads = [output_grad]
        for k in range(1, feats):
            pairs = [((i + k) % feats, i) for i in range(feats)]
            grads.append(lax.ppermute(output_grad, "tp", pairs))
    with jax.named_scope("other_rows"):
        other_matrix = lax.ppermute(output_matrix, "dp", swap)
    dma = pltpu.SemaphoreType.DMA
    with jax.named_scope("local_maps"):
        args = tuple(map(fixed, (queries, key_rows, value_rows, log_decay, write_rate)))
        outs = [far((blocks, 2 * DK, DK), BF16)] + [far(square, BF16)] * 2
        maps, qe, o0 = call(
            local_maps, outs, *args,
            ins=[whole(a) for a in args], out_specs=[whole(o) for o in outs], grid=(1,),
            flops=50 * unit,
        )
    with jax.named_scope("head_grads"):
        maps, head_grad, mine, theirs = call(
            head_grads,
            [far(maps.shape, BF16), shape((BLOCK, wide), BF16)]
            + [shape((BLOCK, rows), BF16)] * 2,
            jnp.stack([core, lax.axis_index("tp")]), *grads,
            fixed(output_matrix), other_matrix, fixed(qe), fixed(maps),
            ins=[SCALAR] + [HELD] * feats + [FAR, HELD, FAR, FAR],
            out_specs=[FAR, HELD, HELD, HELD],
            scratch=[
                pltpu.VMEM((feats,) + output_grad.shape[1:], BF16),
                pltpu.VMEM(output_matrix.shape, BF16),
                pltpu.VMEM(square, BF16),
                pltpu.VMEM((blocks, HALF, DK), BF16),
                dma((2,)),
                dma((2,)),
            ],
            flops=18 * unit,
            input_output_aliases={feats + 4: 0},
        )
        theirs = lax.ppermute(theirs, "dp", swap)
    with jax.named_scope("send_maps"):
        maps = lax.all_to_all(maps, "ctx", 0, 0, tiled=True)
    with jax.named_scope("chain"):
        states, = call(
            chain, [far((blocks, 2 * HALF, DK), BF16)],
            maps, own_half(initial_state), own_half(final_state_grad),
            out_specs=[FAR],
            scratch=[pltpu.VMEM((blocks, 2 * HALF, DK), BF16), dma((blocks, 2))],
            flops=4 * unit,
        )
    with jax.named_scope("return_states"):
        states = lax.all_to_all(states, "ctx", 0, 0, tiled=True)
    with jax.named_scope("outputs"):
        heads_low, = call(
            outputs, [shape((BLOCK, wide), BF16)], qe, o0, states, flops=unit
        )
        other_low = lax.ppermute(heads_low, "dp", swap)
    with jax.named_scope("projection"):
        pieces = (blocks, piece, wide)
        partial, = call(
            projection, [far(pieces, BF16)], mine, theirs, heads_low, other_low,
            out_specs=[FAR], scratch=[pltpu.VMEM(pieces, BF16), dma((4,))], flops=16 * unit,
        )
    with jax.named_scope("gradients"):
        args += (head_grad, states)
        outs = [far(x.shape, x.dtype) for x in args[:5]]
        held = [pltpu.VMEM(x.shape, x.dtype) for x in args + args[:5]] + [dma((12,))]
        *found, partial = call(
            functools.partial(gradients_on, 1), outs + [far(pieces, BF16)],
            core.reshape(1), *args, fixed(partial),
            ins=[SCALAR] + [FAR] * 8, out_specs=[FAR] * 6, scratch=held, flops=35 * unit,
            input_output_aliases={8: 5},
        )
    with jax.named_scope("projection"):
        partial = lax.all_to_all(partial, "ctx", 0, 0, tiled=True)
        spread, = call(
            functools.partial(reduce_spread, float(BLOCK * blocks * lax.axis_size("dp")) ** (-0.5)),
            [far(pieces, BF16)], partial,
            out_specs=[FAR], scratch=[pltpu.VMEM((piece, wide), BF16), dma((blocks, 2))],
        )
        total = lax.all_to_all(spread, "ctx", 0, 0, tiled=True).reshape(rows, wide)
        weight_grad, = call(
            widen, [far((rows, wide), F32)], total,
            out_specs=[FAR], scratch=[pltpu.VMEM((rows, wide), F32), dma((8,))],
        )
    with jax.named_scope("gradients"):
        query_g, key_g, value_g, decay_g, rate_g = call(
            functools.partial(gradients_on, 0), outs,
            core.reshape(1), *args, fixed(spread), *map(fixed, found),
            ins=[SCALAR] + [FAR] * 13, out_specs=[FAR] * 5, scratch=held, flops=35 * unit,
            input_output_aliases={9 + i: i for i in range(5)},
        )
    return (query_g, key_g, value_g, decay_g, rate_g, weight_grad)


def solution(mesh):
    rows = P("dp", "ctx", "tp")
    gates = P("dp", "tp", "ctx")
    state = P("dp", "tp", None, None)
    return jax.shard_map(
        body,
        mesh=mesh,
        in_specs=(rows, rows, rows, gates, gates, state, state, P("dp", "tp"), rows),
        out_specs=(rows, rows, rows, gates, gates, P("dp", "tp")),
        check_vma=False,
    )
```

```python
import functools
import math

import jax
import jax.numpy as jnp
from jax import lax
from jax.experimental import pallas as pl
from jax.experimental.pallas import tpu as pltpu
from jax.sharding import PartitionSpec as P

DK = 128
DV = 128
BLOCK = 128
HALF = DV // 2
F32 = jnp.float32
BF16 = jnp.bfloat16
QSCALE = DK ** (-0.5)

NN = (((1,), (0,)), ((), ()))
NT = (((1,), (1,)), ((), ()))
TN = (((0,), (0,)), ((), ()))


def mm(a, b, dims=NN):
    return lax.dot_general(a.astype(BF16), b.astype(BF16), dims, preferred_element_type=F32)


def split(a):
    high = a.astype(BF16)
    return high, (a - high.astype(F32)).astype(BF16)


def mm3(a, b, dims=NN):
    return mm(a[0], b[0], dims) + (mm(a[0], b[1], dims) + mm(a[1], b[0], dims))


def mm_left(a, b, dims=NN):
    low = b.astype(BF16)
    return mm(a[0], low, dims) + mm(a[1], low, dims)


def mm_right(a, b, dims=NN):
    low = a.astype(BF16)
    return mm(low, b[0], dims) + mm(low, b[1], dims)


def exact(a, b):
    return lax.dot_general(
        a, b, NN, precision=lax.Precision.HIGHEST, preferred_element_type=F32
    )


def iotas():
    row = lax.broadcasted_iota(jnp.int32, (BLOCK, BLOCK), 0)
    col = lax.broadcasted_iota(jnp.int32, (BLOCK, BLOCK), 1)
    return row, col


def unit_rows(rows):
    scale = lax.rsqrt(jnp.sum(rows * rows, axis=-1, keepdims=True) + 1e-06)
    return rows * scale, scale


def gate_columns(gates, row, col):
    cumul = exact(gates, (row <= col).astype(F32))
    columns = cumul.T
    last = columns[BLOCK - 1 : BLOCK, :]
    return cumul, columns, jnp.exp(columns), jnp.exp(last - columns), jnp.exp(last)


def decays(cumul, columns, h, strict):
    gap = columns[:, h : h + 1] - cumul[h : h + 1, :]
    return jnp.where(strict, jnp.exp(jnp.where(strict, gap, 0.0)), 0.0)


def unit_lower_inverses(parts, row, col):
    ident = (row == col).astype(F32)
    found = None
    size = 1
    while size < BLOCK:
        off = (row // (2 * size) == col // (2 * size)) & (row // size != col // size)
        offs = [jnp.where(off, a, 0.0) for a in parts]
        if size == 1:
            found = [ident - a for a in offs]
        else:
            lows = [t.astype(BF16) for t in found]
            inner = [mm(t, a) for t, a in zip(lows, offs)]
            found = [t - mm(x, s) for t, x, s in zip(found, inner, lows)]
        size *= 2
    lows = [t.astype(BF16) for t in found]
    rest = [ident - (t.astype(F32) + mm_left(split(a), t)) for t, a in zip(lows, parts)]
    return [t.astype(F32) + mm(t, r) for t, r in zip(lows, rest)]


class Heads:
    def __init__(self, q_ref, k_ref, g_ref, b_ref):
        self.count = g_ref.shape[1]
        self.copies = self.count * DK // q_ref.shape[2]
        self.row, self.col = iotas()
        self.ident = (self.row == self.col).astype(F32)
        strict = self.row > self.col
        cumul, columns, growth, weight, ends = gate_columns(g_ref[0], self.row, self.col)
        betas = b_ref[0].T
        one = [slice(h, h + 1) for h in range(self.count)]
        self.decay = [decays(cumul, columns, h, strict) for h in range(self.count)]
        self.beta, self.grow, self.keep, self.end = (
            [x[:, cut] for cut in one] for x in (betas, growth, weight, ends)
        )
        self.qn, self.q_scale, self.khat, self.k_scale = [], [], [], []
        self.pair_k, self.pair_q = [], []
        for j in range(self.count // self.copies):
            cut = slice(j * DK, (j + 1) * DK)
            qn, q_scale = unit_rows(q_ref[0, :, cut].astype(F32))
            khat, k_scale = unit_rows(k_ref[0, :, cut].astype(F32))
            self.qn.append(qn)
            self.q_scale.append(q_scale)
            self.khat.append(khat)
            self.k_scale.append(k_scale)
            self.pair_k.append(mm(khat, khat, NT))
            self.pair_q.append(mm(qn * QSCALE, khat, NT))
        parts = [
            self.beta[h] * self.pair_k[h // self.copies] * self.decay[h] for h in range(self.count)
        ]
        self.inverse = [split(t) for t in unit_lower_inverses(parts, self.row, self.col)]


def local_maps(*refs):
    far_in, far_out, held, kept, in_sems, out_sems = (
        refs[:5], refs[5:8], refs[8:13], refs[13:16], *refs[16:]
    )
    fetches = [pltpu.make_async_copy(far_in[i], held[i], in_sems.at[i]) for i in range(5)]
    for copy in fetches:
        copy.start()
    for copy in fetches:
        copy.wait()
    q_ref, k_ref, v_ref, g_ref, b_ref = held
    pay_ref, qe_ref, o0_ref = kept
    x = Heads(q_ref, k_ref, g_ref, b_ref)
    parts = out_sems.shape[0]
    some = x.count // parts
    puts = []
    for h in range(x.count):
        j = h // x.copies
        value = v_ref[0, :, h * DV : (h + 1) * DV].astype(F32)
        wm = mm_left(x.inverse[h], (x.beta[h] * x.grow[h]) * x.khat[j])
        u0 = mm_left(x.inverse[h], x.beta[h] * value)
        kw = split(x.keep[h] * x.khat[j])
        step = (x.end[h] * x.ident - mm_right(wm, kw, TN)).astype(BF16)
        write = mm_right(u0, kw, TN).astype(BF16)
        scores = x.pair_q[j] * (x.decay[h] + x.ident)
        qe_ref[h] = (x.grow[h] * (x.qn[j] * QSCALE) - mm(scores, wm)).astype(BF16)
        o0_ref[h] = mm(scores, u0).astype(BF16)
        for half in range(2):
            pay_ref[2 * h + half, 0:DK] = step
            pay_ref[2 * h + half, DK:] = write[half * HALF : (half + 1) * HALF]
        if (h + 1) % some == 0:
            p, at = h // some, pl.ds(h + 1 - some, some)
            both = pl.ds(2 * (h + 1 - some), 2 * some)
            moves = (
                (pay_ref.at[both], far_out[0].at[both, pl.ds(0, DK + HALF)]),
                (qe_ref.at[at], far_out[1].at[at]),
                (o0_ref.at[at], far_out[2].at[at]),
            )
            for i, (a, b) in enumerate(moves):
                puts.append(pltpu.make_async_copy(a, b, out_sems.at[p, i]))
                puts[-1].start()
    for copy in puts:
        copy.wait()


def gathered_into(all_ref, here, refs):
    for k, ref in enumerate(refs):
        all_ref[lax.rem(here + k, all_ref.shape[0])] = ref[0]


def head_grads(
    at_ref, g0_ref, g1_ref, g2_ref, g3_ref, own_hbm, other_ref, qe_hbm, pay_in,
    pay_ref, hg_ref, all_ref, own_ref, qe_ref, back_ref, in_sems, out_sems,
):
    fetch = pltpu.make_async_copy(own_hbm, own_ref, in_sems.at[0])
    fetch_qe = pltpu.make_async_copy(qe_hbm, qe_ref, in_sems.at[1])
    fetch.start()
    fetch_qe.start()
    core, here = at_ref[0], at_ref[1]
    gathered_into(all_ref, here, (g0_ref, g1_ref, g2_ref, g3_ref))
    feats, wide = all_ref.shape[0], all_ref.shape[2]
    half = feats // 2
    total = jnp.zeros((BLOCK, own_ref.shape[1]), F32)
    for i in range(half):
        total += mm(all_ref[half * (1 - core) + i], other_ref[i * wide : (i + 1) * wide, :])
    fetch.wait()
    for i in range(half):
        total += mm(all_ref[half * core + i], own_ref[i * wide : (i + 1) * wide, :])
    total = total.astype(BF16)
    hg_ref[...] = total
    fetch_qe.wait()
    parts = out_sems.shape[0]
    some = qe_ref.shape[0] // parts
    puts = []
    for p in range(parts):
        for h in range(p * some, (p + 1) * some):
            back = mm(total[:, h * DV : (h + 1) * DV], qe_ref[h], TN).astype(BF16)
            for side in range(2):
                back_ref[2 * h + side] = back[side * HALF : (side + 1) * HALF]
        at = pl.ds(2 * p * some, 2 * some)
        out = pay_ref.at[at, pl.ds(DK + HALF, HALF)]
        puts.append(pltpu.make_async_copy(back_ref.at[at], out, out_sems.at[p]))
        puts[-1].start()
    for copy in puts:
        copy.wait()


def grad_rows(at_ref, g0_ref, g1_ref, g2_ref, g3_ref, mine_ref, theirs_ref, all_ref):
    core, here = at_ref[0], at_ref[1]
    gathered_into(all_ref, here, (g0_ref, g1_ref, g2_ref, g3_ref))
    feats, wide = all_ref.shape[0], all_ref.shape[2]
    half = feats // 2
    for i in range(half):
        cut = slice(i * wide, (i + 1) * wide)
        mine_ref[cut, :] = all_ref[half * core + i].T
        theirs_ref[cut, :] = all_ref[half * (1 - core) + i].T


def chain(maps_ref, first_ref, last_ref, out_ref, kept_ref, sems):
    blocks = maps_ref.shape[0]
    some = blocks // sems.shape[0]
    copies = []

    def times(state, step, dims):
        out = mm(jnp.concatenate(split(state), axis=0), step, dims)
        return out[:HALF] + out[HALF:]

    def send(first, side):
        at = (pl.ds(first, some), pl.ds(side * HALF, HALF))
        group = sems.at[first // some, side]
        copies.append(pltpu.make_async_copy(kept_ref.at[at], out_ref.at[at], group))
        copies[-1].start()

    state, back = first_ref[...], last_ref[...]
    for c in range(blocks):
        e = blocks - 1 - c
        kept_ref[c, 0:HALF] = state.astype(BF16)
        kept_ref[e, HALF:] = back.astype(BF16)
        if (c + 1) % some == 0:
            send(c + 1 - some, 0)
            send(e, 1)
        if c < blocks - 1:
            write = maps_ref[c, DK : DK + HALF].astype(F32)
            read = maps_ref[e, DK + HALF :].astype(F32)
            state = times(state, maps_ref[c, 0:DK], NN) + write
            back = times(back, maps_ref[e, 0:DK], NT) + read
    for copy in copies:
        copy.wait()


def projection(mine_ref, theirs_ref, low_ref, other_ref, out_ref, kept_ref, sems):
    blocks, piece = out_ref.shape[0], out_ref.shape[1]
    parts = sems.shape[0]
    some = blocks // parts
    lows = jnp.concatenate([low_ref[...], other_ref[...]], axis=0)
    copies = []
    for p in range(parts):
        cut = slice(p * some * piece, (p + 1) * some * piece)
        rows = jnp.concatenate([mine_ref[cut, :], theirs_ref[cut, :]], axis=1)
        total = mm(rows, lows).astype(BF16)
        for c in range(some):
            kept_ref[p * some + c] = total[c * piece : (c + 1) * piece]
        at = pl.ds(p * some, some)
        copies.append(pltpu.make_async_copy(kept_ref.at[at], out_ref.at[at], sems.at[p]))
        copies[-1].start()
    for copy in copies:
        copy.wait()


def reduce_spread(scale, pieces_ref, out_ref, sum_ref, sems):
    blocks, rows = out_ref.shape[:2]
    parts = sems.shape[1]
    copies = []
    for p in range(parts):
        at = pl.ds(p * (rows // parts), rows // parts)
        total = pieces_ref[0, at].astype(F32)
        for c in range(1, blocks):
            total += pieces_ref[c, at].astype(F32)
        sum_ref[at] = (total * scale).astype(BF16)
        for c in range(blocks):
            copy = pltpu.make_async_copy(sum_ref.at[at], out_ref.at[c, at], sems.at[c, p])
            copy.start()
            copies.append(copy)
    for copy in copies:
        copy.wait()


def widen(in_ref, out_ref, kept_ref, sems):
    parts = sems.shape[0]
    step = in_ref.shape[0] // parts
    copies = []
    for p in range(parts):
        at = pl.ds(p * step, step)
        kept_ref[at, :] = in_ref[at, :].astype(F32)
        copies.append(pltpu.make_async_copy(kept_ref.at[at], out_ref.at[at], sems.at[p]))
        copies[-1].start()
    for copy in copies:
        copy.wait()


def halves_of(ref, h, low):
    rows = slice(low, low + HALF)
    return jnp.concatenate([ref[2 * h, rows], ref[2 * h + 1, rows]], axis=0)


def outputs(qe_ref, o0_ref, y_ref, o_ref):
    for h in range(qe_ref.shape[0]):
        out = o0_ref[h].astype(F32) + mm(qe_ref[h], halves_of(y_ref, h, 0), NT)
        o_ref[:, h * DV : (h + 1) * DV] = out.astype(BF16)


def gradients(
    q_ref, k_ref, v_ref, g_ref, b_ref, hg_ref, y_ref,
    dq_ref, dk_ref, dv_ref, dg_ref, db_ref,
):
    x = Heads(q_ref, k_ref, g_ref, b_ref)
    row, col = x.row, x.col
    strict = row > col
    lane = lax.broadcasted_iota(jnp.int32, (BLOCK, x.count), 1)
    level = lax.broadcasted_iota(jnp.int32, (x.count, BLOCK), 0)
    cumul_g = jnp.zeros((BLOCK, x.count), F32)
    beta_g = jnp.zeros((BLOCK, x.count), F32)
    across = jnp.zeros((x.count, BLOCK), F32)
    for j in range(x.count // x.copies):
        cut = slice(j * DK, (j + 1) * DK)
        qn, khat = x.qn[j], x.khat[j]
        qhat = qn * QSCALE
        qlow, klow = qhat.astype(BF16), khat.astype(BF16)
        pair_k, pair_q = x.pair_k[j], x.pair_q[j]
        qhat_g = jnp.zeros((BLOCK, DK), F32)
        khat_g = jnp.zeros((BLOCK, DK), F32)
        for h in range(j * x.copies, (j + 1) * x.copies):
            cut_v = slice(h * DV, (h + 1) * DV)
            decay, grow, keep, beta = x.decay[h], x.grow[h], x.keep[h], x.beta[h]
            value = v_ref[0, :, cut_v].astype(F32)
            state, back = halves_of(y_ref, h, 0), halves_of(y_ref, h, HALF)
            out_g = hg_ref[:, cut_v]
            decay_in = decay + x.ident
            scores = pair_q * decay_in
            inverse = x.inverse[h]
            known = beta * (value - grow * mm_left(split(khat), state, NT))
            fresh = split(mm3(inverse, split(known)))
            fresh_g = mm_left(split(scores), out_g, TN) + mm_left(split(keep * khat), back, NT)
            rhs_g = mm3(inverse, split(fresh_g), TN)
            rhs = split(rhs_g)
            read_q = mm(out_g, state)
            read_k = mm_left(rhs, state)
            scores_g = mm_right(out_g, fresh, NT)
            part_g = jnp.where(strict, -mm3(rhs, fresh, NT), 0.0) * decay
            pair_qg, pair_kg = split(scores_g * decay_in), split(part_g * beta)
            kept_g = mm_left(fresh, back)
            part_k = part_g * pair_k
            gaps = scores_g * scores + part_k * beta
            low_q = mm_left(pair_qg, klow).astype(BF16).astype(F32)
            low_k = mm_left(pair_qg, qlow, TN) + mm_left(pair_kg, klow)
            low_k += mm_left(pair_kg, klow, TN)
            qhat_g += grow * read_q + low_q
            khat_g += keep * kept_g - (beta * grow) * read_k + low_k.astype(BF16).astype(F32)
            dv_ref[0, :, cut_v] = (beta * rhs_g).astype(BF16)
            read_sum = jnp.sum(read_k * khat, axis=1, keepdims=True)
            beta_col = jnp.sum(rhs_g * value + part_k, axis=1, keepdims=True) - grow * read_sum
            kept_sum = jnp.sum(kept_g * khat, axis=1, keepdims=True) * keep
            grow_g = jnp.sum(read_q * qhat, axis=1, keepdims=True) - beta * read_sum
            cumul_col = grow_g * grow + jnp.sum(gaps, axis=1, keepdims=True) - kept_sum
            whole = jnp.sum(back.astype(F32) * state.astype(F32)) * x.end[h]
            at_end = jnp.sum(kept_sum, axis=0, keepdims=True) + whole
            cumul_col += jnp.where(row[:, 0:1] == BLOCK - 1, at_end, 0.0)
            cumul_g = jnp.where(lane == h, cumul_col, cumul_g)
            beta_g = jnp.where(lane == h, beta_col, beta_g)
            across = jnp.where(level == h, jnp.sum(gaps, axis=0, keepdims=True), across)
        q_along = jnp.sum(qn * qhat_g, axis=1, keepdims=True)
        k_along = jnp.sum(khat * khat_g, axis=1, keepdims=True)
        dq_ref[0, :, cut] = ((x.q_scale[j] * QSCALE) * (qhat_g - qn * q_along)).astype(BF16)
        dk_ref[0, :, cut] = (x.k_scale[j] * (khat_g - khat * k_along)).astype(BF16)
    db_ref[0] = beta_g.T
    dg_ref[0] = exact(cumul_g.T - across, (row >= col).astype(F32))


def gradients_on(turn, at_ref, *refs):
    *held, sems = refs[-13:]
    far_in = refs[:7]
    far_out = refs[7 + (1 if turn else 6) :][:5]

    @pl.when(at_ref[0] == turn)
    def _():
        fetches = [pltpu.make_async_copy(far_in[i], held[i], sems.at[i]) for i in range(7)]
        for copy in fetches:
            copy.start()
        for copy in fetches:
            copy.wait()
        gradients(*held)
        puts = [pltpu.make_async_copy(held[7 + i], far_out[i], sems.at[7 + i]) for i in range(5)]
        for copy in puts:
            copy.start()
        for copy in puts:
            copy.wait()


def whole(x):
    return pl.BlockSpec(x.shape, lambda *i: (0,) * len(x.shape))


SCALAR = pl.BlockSpec(memory_space=pltpu.SMEM)
HELD = pl.BlockSpec(memory_space=pltpu.VMEM)
FAR = pl.BlockSpec(memory_space=pl.ANY)


def call(kernel, outs, *args, ins=None, out_specs=None, flops=0, scratch=(), grid=(), limit=24, **more):
    size = sum(math.prod(x.shape) * x.dtype.itemsize for x in (*args, *outs))
    return pl.pallas_call(
        kernel,
        grid=grid,
        out_shape=outs,
        in_specs=[HELD] * len(args) if ins is None else ins,
        out_specs=[HELD] * len(outs) if out_specs is None else out_specs,
        scratch_shapes=scratch,
        compiler_params=pltpu.CompilerParams(vmem_limit_bytes=limit * 2**20),
        cost_estimate=pl.CostEstimate(flops=flops, bytes_accessed=size, transcendentals=0),
        **more,
    )(*args)


def shape(dims, dtype):
    return jax.ShapeDtypeStruct(dims, dtype)


def far(dims, dtype):
    return pltpu.HBM(dims, dtype)


def fixed(x):
    return pltpu.with_memory_space_constraint(x, pltpu.HBM)


def body(
    queries, key_rows, value_rows, log_decay, write_rate,
    initial_state, final_state_grad, output_matrix, output_grad,
):
    heads = log_decay.shape[1]
    blocks = lax.axis_size("ctx")
    feats = lax.axis_size("tp")
    here, core = lax.axis_index("ctx"), lax.axis_index("dp")
    rows, wide = output_matrix.shape
    piece = rows // blocks
    swap = [(0, 1), (1, 0)]
    square = (heads, BLOCK, DK)
    unit = 2 * BLOCK**3 * heads

    def own_half(states):
        parts = states.reshape(blocks, HALF, DK)
        return lax.dynamic_index_in_dim(parts, here, 0, keepdims=False)

    with jax.named_scope("gather_grad"):
        grads = [output_grad]
        for k in range(1, feats):
            pairs = [((i + k) % feats, i) for i in range(feats)]
            grads.append(lax.ppermute(output_grad, "tp", pairs))
    with jax.named_scope("other_rows"):
        other_matrix = lax.ppermute(output_matrix, "dp", swap)
    dma = pltpu.SemaphoreType.DMA
    with jax.named_scope("local_maps"):
        args = tuple(map(fixed, (queries, key_rows, value_rows, log_decay, write_rate)))
        outs = [far((blocks, 2 * DK, DK), BF16)] + [far(square, BF16)] * 2
        maps, qe, o0 = call(
            local_maps, outs, *args,
            ins=[FAR] * 5, out_specs=[FAR] * 3,
            scratch=[pltpu.VMEM(x.shape, x.dtype) for x in args]
            + [pltpu.VMEM((blocks, DK + HALF, DK), BF16)]
            + [pltpu.VMEM(square, BF16)] * 2
            + [dma((5,)), dma((2, 3))],
            flops=50 * unit,
        )
    with jax.named_scope("head_grads"):
        place = jnp.stack([core, lax.axis_index("tp")])
        gather = pltpu.VMEM((feats,) + output_grad.shape[1:], BF16)
        maps, head_grad = call(
            head_grads,
            [far(maps.shape, BF16), shape((BLOCK, wide), BF16)],
            place, *grads, fixed(output_matrix), other_matrix, fixed(qe), fixed(maps),
            ins=[SCALAR] + [HELD] * feats + [FAR, HELD, FAR, FAR],
            out_specs=[FAR, HELD],
            scratch=[
                gather,
                pltpu.VMEM(output_matrix.shape, BF16),
                pltpu.VMEM(square, BF16),
                pltpu.VMEM((blocks, HALF, DK), BF16),
                dma((2,)),
                dma((2,)),
            ],
            flops=18 * unit,
            input_output_aliases={feats + 4: 0},
        )
    with jax.named_scope("send_maps"):
        maps = lax.all_to_all(maps, "ctx", 0, 0, tiled=True)
    with jax.named_scope("grad_rows"):
        mine, theirs = call(
            grad_rows, [shape((rows, BLOCK), BF16)] * 2, place, *grads,
            ins=[SCALAR] + [HELD] * feats, scratch=[gather],
        )
        theirs = lax.ppermute(theirs, "dp", swap)
    with jax.named_scope("chain"):
        states, = call(
            chain, [far((blocks, 2 * HALF, DK), BF16)],
            maps, own_half(initial_state), own_half(final_state_grad),
            out_specs=[FAR],
            scratch=[pltpu.VMEM((blocks, 2 * HALF, DK), BF16), dma((4, 2))],
            flops=4 * unit,
        )
    with jax.named_scope("return_states"):
        states = lax.all_to_all(states, "ctx", 0, 0, tiled=True)
    with jax.named_scope("outputs"):
        heads_low, = call(
            outputs, [shape((BLOCK, wide), BF16)], qe, o0, states, flops=unit
        )
        other_low = lax.ppermute(heads_low, "dp", swap)
    with jax.named_scope("projection"):
        pieces = (blocks, piece, wide)
        partial, = call(
            projection, [far(pieces, BF16)], mine, theirs, heads_low, other_low,
            out_specs=[FAR], scratch=[pltpu.VMEM(pieces, BF16), dma((4,))], flops=16 * unit,
        )
    with jax.named_scope("gradients"):
        args += (head_grad, states)
        outs = [far(x.shape, x.dtype) for x in args[:5]]
        held = [pltpu.VMEM(x.shape, x.dtype) for x in args + args[:5]] + [dma((12,))]
        *found, partial = call(
            functools.partial(gradients_on, 1), outs + [far(pieces, BF16)],
            core.reshape(1), *args, fixed(partial),
            ins=[SCALAR] + [FAR] * 8, out_specs=[FAR] * 6, scratch=held, flops=35 * unit,
            input_output_aliases={8: 5},
        )
    with jax.named_scope("projection"):
        partial = lax.all_to_all(partial, "ctx", 0, 0, tiled=True)
        spread, = call(
            functools.partial(reduce_spread, float(BLOCK * blocks * lax.axis_size("dp")) ** (-0.5)),
            [far(pieces, BF16)], partial,
            out_specs=[FAR], scratch=[pltpu.VMEM((piece, wide), BF16), dma((blocks, 2))],
        )
        total = lax.all_to_all(spread, "ctx", 0, 0, tiled=True).reshape(rows, wide)
        weight_grad, = call(
            widen, [far((rows, wide), F32)], total,
            out_specs=[FAR], scratch=[pltpu.VMEM((rows, wide), F32), dma((8,))],
        )
    with jax.named_scope("gradients"):
        query_g, key_g, value_g, decay_g, rate_g = call(
            functools.partial(gradients_on, 0), outs,
            core.reshape(1), *args, fixed(spread), *map(fixed, found),
            ins=[SCALAR] + [FAR] * 13, out_specs=[FAR] * 5, scratch=held, flops=35 * unit,
            input_output_aliases={9 + i: i for i in range(5)},
        )
    return (query_g, key_g, value_g, decay_g, rate_g, weight_grad)


def solution(mesh):
    rows = P("dp", "ctx", "tp")
    gates = P("dp", "tp", "ctx")
    state = P("dp", "tp", None, None)
    return jax.shard_map(
        body,
        mesh=mesh,
        in_specs=(rows, rows, rows, gates, gates, state, state, P("dp", "tp"), rows),
        out_specs=(rows, rows, rows, gates, gates, P("dp", "tp")),
        check_vma=False,
    )
```

```python
import functools
import math

import jax
import jax.numpy as jnp
from jax import lax
from jax.experimental import pallas as pl
from jax.experimental.pallas import tpu as pltpu
from jax.sharding import PartitionSpec as P

DK = 128
DV = 128
BLOCK = 128
HALF = DV // 2
F32 = jnp.float32
BF16 = jnp.bfloat16
QSCALE = DK ** (-0.5)

NN = (((1,), (0,)), ((), ()))
NT = (((1,), (1,)), ((), ()))
TN = (((0,), (0,)), ((), ()))


def mm(a, b, dims=NN):
    return lax.dot_general(a.astype(BF16), b.astype(BF16), dims, preferred_element_type=F32)


def split(a):
    high = a.astype(BF16)
    return high, (a - high.astype(F32)).astype(BF16)


def mm3(a, b, dims=NN):
    return mm(a[0], b[0], dims) + (mm(a[0], b[1], dims) + mm(a[1], b[0], dims))


def mm_left(a, b, dims=NN):
    low = b.astype(BF16)
    return mm(a[0], low, dims) + mm(a[1], low, dims)


def mm_right(a, b, dims=NN):
    low = a.astype(BF16)
    return mm(low, b[0], dims) + mm(low, b[1], dims)


def exact(a, b):
    return lax.dot_general(
        a, b, NN, precision=lax.Precision.HIGHEST, preferred_element_type=F32
    )


def iotas():
    row = lax.broadcasted_iota(jnp.int32, (BLOCK, BLOCK), 0)
    col = lax.broadcasted_iota(jnp.int32, (BLOCK, BLOCK), 1)
    return row, col


def unit_rows(rows):
    scale = lax.rsqrt(jnp.sum(rows * rows, axis=-1, keepdims=True) + 1e-06)
    return rows * scale, scale


def gate_columns(gates, row, col):
    cumul = exact(gates, (row <= col).astype(F32))
    columns = cumul.T
    last = columns[BLOCK - 1 : BLOCK, :]
    return cumul, columns, jnp.exp(columns), jnp.exp(last - columns), jnp.exp(last)


def decays(cumul, columns, h, strict):
    gap = columns[:, h : h + 1] - cumul[h : h + 1, :]
    return jnp.where(strict, jnp.exp(jnp.where(strict, gap, 0.0)), 0.0)


def unit_lower_inverses(parts, row, col, finer):
    ident = (row == col).astype(F32)
    found = None
    size = 1
    while size < BLOCK:
        off = (row // (2 * size) == col // (2 * size)) & (row // size != col // size)
        offs = [jnp.where(off, a, 0.0) for a in parts]
        if size == 1:
            found = [ident - a for a in offs]
        else:
            lows = [t.astype(BF16) for t in found]
            inner = [mm(t, a) for t, a in zip(lows, offs)]
            found = [t - mm(x, s) for t, x, s in zip(found, inner, lows)]
        size *= 2
    lows = [t.astype(BF16) for t in found]
    rest = [ident - (t.astype(F32) + mm_left(split(a), t)) for t, a in zip(lows, parts)]
    found = [t.astype(F32) + mm(t, r) for t, r in zip(lows, rest)]
    if finer:
        rest = [ident - (t + mm3(split(a), split(t))) for t, a in zip(found, parts)]
        found = [t + mm3(split(t), split(r)) for t, r in zip(found, rest)]
    return found


class Heads:
    def __init__(self, q_ref, k_ref, g_ref, b_ref, inverse=None, finer=False):
        self.count = g_ref.shape[1]
        self.copies = self.count * DK // q_ref.shape[2]
        self.row, self.col = iotas()
        self.ident = (self.row == self.col).astype(F32)
        strict = self.row > self.col
        cumul, columns, growth, weight, ends = gate_columns(g_ref[0], self.row, self.col)
        betas = b_ref[0].T
        one = [slice(h, h + 1) for h in range(self.count)]
        self.decay = [decays(cumul, columns, h, strict) for h in range(self.count)]
        self.beta, self.grow, self.keep, self.end = (
            [x[:, cut] for cut in one] for x in (betas, growth, weight, ends)
        )
        self.qn, self.q_scale, self.khat, self.k_scale = [], [], [], []
        self.pair_k, self.pair_q = [], []
        for j in range(self.count // self.copies):
            cut = slice(j * DK, (j + 1) * DK)
            qn, q_scale = unit_rows(q_ref[0, :, cut].astype(F32))
            khat, k_scale = unit_rows(k_ref[0, :, cut].astype(F32))
            self.qn.append(qn)
            self.q_scale.append(q_scale)
            self.khat.append(khat)
            self.k_scale.append(k_scale)
            self.pair_k.append(mm(khat, khat, NT))
            self.pair_q.append(mm(qn * QSCALE, khat, NT))
        self.inverse = inverse
        if inverse is None:
            parts = [
                self.beta[h] * self.pair_k[h // self.copies] * self.decay[h]
                for h in range(self.count)
            ]
            found = unit_lower_inverses(parts, self.row, self.col, finer)
            self.inverse = [split(t) for t in found]

    def fresh(self, h, value, state):
        read = mm_left(split(self.khat[h // self.copies]), state, NT)
        return split(mm3(self.inverse[h], split(self.beta[h] * (value - self.grow[h] * read))))


def local_maps(*refs):
    far_in, far_out, held, kept, in_sems, out_sems = (
        refs[:5], refs[5:8], refs[8:13], refs[13:16], *refs[16:]
    )
    fetches = [pltpu.make_async_copy(far_in[i], held[i], in_sems.at[i]) for i in range(5)]
    for copy in fetches:
        copy.start()
    for copy in fetches:
        copy.wait()
    q_ref, k_ref, v_ref, g_ref, b_ref = held
    pay_ref, qe_ref, o0_ref = kept
    x = Heads(q_ref, k_ref, g_ref, b_ref)
    parts = out_sems.shape[0]
    some = x.count // parts
    puts = []
    for h in range(x.count):
        j = h // x.copies
        value = v_ref[0, :, h * DV : (h + 1) * DV].astype(F32)
        wm = mm_left(x.inverse[h], (x.beta[h] * x.grow[h]) * x.khat[j])
        u0 = mm_left(x.inverse[h], x.beta[h] * value)
        kw = split(x.keep[h] * x.khat[j])
        step = (x.end[h] * x.ident - mm_right(wm, kw, TN)).astype(BF16)
        write = mm_right(u0, kw, TN).astype(BF16)
        scores = x.pair_q[j] * (x.decay[h] + x.ident)
        qe_ref[h] = (x.grow[h] * (x.qn[j] * QSCALE) - mm(scores, wm)).astype(BF16)
        o0_ref[h] = mm(scores, u0).astype(BF16)
        for half in range(2):
            pay_ref[2 * h + half, 0:DK] = step
            pay_ref[2 * h + half, DK:] = write[half * HALF : (half + 1) * HALF]
        if (h + 1) % some == 0:
            p, at = h // some, pl.ds(h + 1 - some, some)
            both = pl.ds(2 * (h + 1 - some), 2 * some)
            moves = (
                (pay_ref.at[both], far_out[0].at[both]),
                (qe_ref.at[at], far_out[1].at[at]),
                (o0_ref.at[at], far_out[2].at[at]),
            )
            for i, (a, b) in enumerate(moves):
                puts.append(pltpu.make_async_copy(a, b, out_sems.at[p, i]))
                puts[-1].start()
    for copy in puts:
        copy.wait()


def gathered_into(all_ref, here, refs):
    for k, ref in enumerate(refs):
        all_ref[lax.rem(here + k, all_ref.shape[0])] = ref[0]


def head_grads(
    at_ref, g0_ref, g1_ref, g2_ref, g3_ref, own_hbm, other_ref, qe_hbm,
    back_out, hg_ref, all_ref, own_ref, qe_ref, back_ref, in_sems, out_sems,
):
    fetch = pltpu.make_async_copy(own_hbm, own_ref, in_sems.at[0])
    fetch_qe = pltpu.make_async_copy(qe_hbm, qe_ref, in_sems.at[1])
    fetch.start()
    fetch_qe.start()
    core, here = at_ref[0], at_ref[1]
    gathered_into(all_ref, here, (g0_ref, g1_ref, g2_ref, g3_ref))
    feats, wide = all_ref.shape[0], all_ref.shape[2]
    half = feats // 2
    total = jnp.zeros((BLOCK, own_ref.shape[1]), F32)
    for i in range(half):
        total += mm(all_ref[half * (1 - core) + i], other_ref[i * wide : (i + 1) * wide, :])
    fetch.wait()
    for i in range(half):
        total += mm(all_ref[half * core + i], own_ref[i * wide : (i + 1) * wide, :])
    total = total.astype(BF16)
    hg_ref[...] = total
    fetch_qe.wait()
    parts = out_sems.shape[0]
    some = qe_ref.shape[0] // parts
    puts = []
    for p in range(parts):
        for h in range(p * some, (p + 1) * some):
            back = mm(total[:, h * DV : (h + 1) * DV], qe_ref[h], TN).astype(BF16)
            for side in range(2):
                back_ref[2 * h + side] = back[side * HALF : (side + 1) * HALF]
        at = pl.ds(2 * p * some, 2 * some)
        puts.append(pltpu.make_async_copy(back_ref.at[at], back_out.at[at], out_sems.at[p]))
        puts[-1].start()
    for copy in puts:
        copy.wait()


def grad_rows(at_ref, g0_ref, g1_ref, g2_ref, g3_ref, mine_ref, theirs_ref, all_ref):
    core, here = at_ref[0], at_ref[1]
    gathered_into(all_ref, here, (g0_ref, g1_ref, g2_ref, g3_ref))
    feats, wide = all_ref.shape[0], all_ref.shape[2]
    half = feats // 2
    for i in range(half):
        cut = slice(i * wide, (i + 1) * wide)
        mine_ref[cut, :] = all_ref[half * core + i].T
        theirs_ref[cut, :] = all_ref[half * (1 - core) + i].T


def times(state, step, dims):
    out = mm(jnp.concatenate(split(state), axis=0), step, dims)
    return out[:HALF] + out[HALF:]


def forward_chain(
    at_ref, maps_hbm, back_hbm, first_hbm, out_ref,
    maps_ref, kept_ref, first_ref, back_sems, in_sems, sems,
):
    blocks, parts = maps_ref.shape[0], sems.shape[0]
    some = blocks // parts
    groups = [pl.ds(p * some, some) for p in range(parts)]
    fetches = [
        pltpu.make_async_copy(maps_hbm.at[at], maps_ref.at[at], in_sems.at[p])
        for p, at in enumerate(groups)
    ]
    fetch_first = pltpu.make_async_copy(first_hbm.at[at_ref[0]], first_ref, back_sems.at[1])
    fetch_first.start()
    fetches[0].start()
    fetch_back = pltpu.make_async_copy(back_hbm, kept_ref.at[:, pl.ds(HALF, HALF)], back_sems.at[0])
    fetch_back.start()
    for copy in fetches[1:]:
        copy.start()
    copies = []
    fetch_first.wait()
    state = first_ref[...]
    for c in range(blocks):
        kept_ref[c, 0:HALF] = state.astype(BF16)
        if c % some == 0:
            fetches[c // some].wait()
        if (c + 1) % some == 0:
            p = c // some
            if p == 0:
                fetch_back.wait()
            at = groups[p]
            copies.append(pltpu.make_async_copy(kept_ref.at[at], out_ref.at[at], sems.at[p]))
            copies[-1].start()
        if c < blocks - 1:
            state = times(state, maps_ref[c, 0:DK], NN) + maps_ref[c, DK:].astype(F32)
    for copy in copies:
        copy.wait()


def backward_chain(
    at_ref, maps_hbm, in_ref, last_hbm, out_ref, maps_ref, kept_ref, last_ref, last_sem, in_sems, sems
):
    blocks, parts = maps_ref.shape[0], sems.shape[0]
    some = blocks // parts
    wide = out_ref.shape[2] - DK
    groups = [pl.ds(p * some, some) for p in range(parts)]
    fetches = [
        pltpu.make_async_copy(maps_hbm.at[at, pl.ds(0, DK)], maps_ref.at[at], in_sems.at[p])
        for p, at in enumerate(groups)
    ]
    fetch_last = pltpu.make_async_copy(last_hbm.at[at_ref[0]], last_ref, last_sem)
    fetch_last.start()
    for copy in reversed(fetches):
        copy.start()
    copies = []
    fetch_last.wait()
    back = last_ref[...]
    for c in range(blocks - 1, -1, -1):
        kept_ref[c] = back.astype(BF16)
        p = c // some
        if c % some == some - 1:
            fetches[p].wait()
        if c % some == 0:
            out = out_ref.at[groups[p], :, pl.ds(wide, DK)]
            copies.append(pltpu.make_async_copy(kept_ref.at[groups[p]], out, sems.at[p]))
            copies[-1].start()
        if c > 0:
            back = times(back, maps_ref[c], NT) + in_ref[c, HALF:].astype(F32)
    for copy in copies:
        copy.wait()


def projection(mine_ref, theirs_ref, low_ref, other_ref, in_ref, out_ref, kept_ref, sems):
    blocks, piece, wide = kept_ref.shape
    parts = sems.shape[0]
    some = blocks // parts
    lows = jnp.concatenate([low_ref[...], other_ref[...]], axis=0)
    copies = []
    for p in range(parts):
        cut = slice(p * some * piece, (p + 1) * some * piece)
        rows = jnp.concatenate([mine_ref[cut, :], theirs_ref[cut, :]], axis=1)
        total = mm(rows, lows).astype(BF16)
        for c in range(some):
            kept_ref[p * some + c] = total[c * piece : (c + 1) * piece]
        at = pl.ds(p * some, some)
        out = out_ref.at[at, :, pl.ds(0, wide)]
        copies.append(pltpu.make_async_copy(kept_ref.at[at], out, sems.at[p]))
        copies[-1].start()
    for copy in copies:
        copy.wait()


def reduce_spread(scale, pieces_ref, out_ref, back_ref, sum_ref, back_sem, sems):
    blocks, rows, wide = out_ref.shape
    parts = sems.shape[1]
    copies = []
    for p in range(parts):
        at = pl.ds(p * (rows // parts), rows // parts)
        total = pieces_ref[0, at, 0:wide].astype(F32)
        for c in range(1, blocks):
            total += pieces_ref[c, at, 0:wide].astype(F32)
        sum_ref[at] = (total * scale).astype(BF16)
        for c in range(blocks):
            copy = pltpu.make_async_copy(sum_ref.at[at], out_ref.at[c, at], sems.at[c, p])
            copy.start()
            copies.append(copy)
    back = pieces_ref.at[:, :, pl.ds(wide, DK)]
    copies.append(pltpu.make_async_copy(back, back_ref, back_sem))
    copies[-1].start()
    for copy in copies:
        copy.wait()


def widen(in_ref, out_ref, kept_ref, sems):
    parts = sems.shape[0]
    step = in_ref.shape[0] // parts
    copies = []
    for p in range(parts):
        at = pl.ds(p * step, step)
        kept_ref[at, :] = in_ref[at, :].astype(F32)
        copies.append(pltpu.make_async_copy(kept_ref.at[at], out_ref.at[at], sems.at[p]))
        copies[-1].start()
    for copy in copies:
        copy.wait()


def halves_of(ref, h, low):
    rows = slice(low, low + HALF)
    return jnp.concatenate([ref[2 * h, rows], ref[2 * h + 1, rows]], axis=0)


def outputs(qe_ref, o0_ref, y_ref, o_ref):
    for h in range(qe_ref.shape[0]):
        out = o0_ref[h].astype(F32) + mm(qe_ref[h], halves_of(y_ref, h, 0), NT)
        o_ref[:, h * DV : (h + 1) * DV] = out.astype(BF16)


def query_gradients(
    q_ref, k_ref, v_ref, g_ref, b_ref, hg_ref, y_ref, dq_ref, dk_ref, dg_ref, rhs_ref,
    *kept_refs,
):
    x = Heads(q_ref, k_ref, g_ref, b_ref, finer=True)
    lane = lax.broadcasted_iota(jnp.int32, (BLOCK, x.count), 1)
    level = lax.broadcasted_iota(jnp.int32, (x.count, BLOCK), 0)
    cumul_g = jnp.zeros((BLOCK, x.count), F32)
    across = jnp.zeros((x.count, BLOCK), F32)
    for j in range(x.count // x.copies):
        cut = slice(j * DK, (j + 1) * DK)
        qn, klow = x.qn[j], x.khat[j].astype(BF16)
        qhat = qn * QSCALE
        qlow = qhat.astype(BF16)
        qhat_g = jnp.zeros((BLOCK, DK), F32)
        khat_g = jnp.zeros((BLOCK, DK), F32)
        for h in range(j * x.copies, (j + 1) * x.copies):
            cut_v = slice(h * DV, (h + 1) * DV)
            value = v_ref[0, :, cut_v].astype(F32)
            state, out_g = halves_of(y_ref, h, 0), hg_ref[:, cut_v]
            decay_in = x.decay[h] + x.ident
            fresh = x.fresh(h, value, state)
            for ref, part in zip(kept_refs, (*x.inverse[h], *fresh)):
                ref[h] = part
            pair_g = mm_right(out_g, fresh, NT) * decay_in
            gaps = pair_g * x.pair_q[j]
            pair_g = split(pair_g)
            scores = x.pair_q[j] * decay_in
            fresh_g = mm_left(split(scores), out_g, TN)
            rhs_ref[h] = mm3(x.inverse[h], split(fresh_g), TN)
            read_q = mm(out_g, state)
            low_q, low_k = mm_left(pair_g, klow), mm_left(pair_g, qlow, TN)
            qhat_g += x.grow[h] * read_q + low_q.astype(BF16).astype(F32)
            khat_g += low_k.astype(BF16).astype(F32)
            grow_g = jnp.sum(read_q * qhat, axis=1, keepdims=True)
            cumul_col = grow_g * x.grow[h] + jnp.sum(gaps, axis=1, keepdims=True)
            cumul_g = jnp.where(lane == h, cumul_col, cumul_g)
            across = jnp.where(level == h, jnp.sum(gaps, axis=0, keepdims=True), across)
        q_along = jnp.sum(qn * qhat_g, axis=1, keepdims=True)
        dq_ref[0, :, cut] = ((x.q_scale[j] * QSCALE) * (qhat_g - qn * q_along)).astype(BF16)
        dk_ref[0, :, cut] = khat_g
    dg_ref[0] = cumul_g.T - across


def gradients(
    q_ref, k_ref, v_ref, g_ref, b_ref, hg_ref, y_ref, back_ref, part_dk_ref, part_dg_ref,
    part_rhs_ref, t_high_ref, t_low_ref, fresh_high_ref, fresh_low_ref,
    dk_ref, dv_ref, dg_ref, db_ref,
):
    inverse = [(t_high_ref[h], t_low_ref[h]) for h in range(g_ref.shape[1])]
    x = Heads(q_ref, k_ref, g_ref, b_ref, inverse)
    row, col = x.row, x.col
    strict = row > col
    lane = lax.broadcasted_iota(jnp.int32, (BLOCK, x.count), 1)
    level = lax.broadcasted_iota(jnp.int32, (x.count, BLOCK), 0)
    cumul_g = jnp.zeros((BLOCK, x.count), F32)
    beta_g = jnp.zeros((BLOCK, x.count), F32)
    across = jnp.zeros((x.count, BLOCK), F32)
    for j in range(x.count // x.copies):
        cut = slice(j * DK, (j + 1) * DK)
        khat = x.khat[j]
        klow = khat.astype(BF16)
        pair_k = x.pair_k[j]
        khat_g = part_dk_ref[0, :, cut]
        for h in range(j * x.copies, (j + 1) * x.copies):
            cut_v = slice(h * DV, (h + 1) * DV)
            decay, grow, keep, beta = x.decay[h], x.grow[h], x.keep[h], x.beta[h]
            value = v_ref[0, :, cut_v].astype(F32)
            state, back = halves_of(y_ref, h, 0), halves_of(back_ref, h, 0)
            fresh = fresh_high_ref[h], fresh_low_ref[h]
            fresh_g = mm_left(split(keep * khat), back, NT)
            rhs_g = part_rhs_ref[h] + mm3(x.inverse[h], split(fresh_g), TN)
            rhs = split(rhs_g)
            read_k = mm_left(rhs, state)
            part_g = jnp.where(strict, -mm3(rhs, fresh, NT), 0.0) * decay
            pair_kg = split(part_g * beta)
            kept_g = mm_left(fresh, back)
            part_k = part_g * pair_k
            gaps = part_k * beta
            low_k = mm_left(pair_kg, klow) + mm_left(pair_kg, klow, TN)
            khat_g += keep * kept_g - (beta * grow) * read_k + low_k.astype(BF16).astype(F32)
            dv_ref[0, :, cut_v] = (beta * rhs_g).astype(BF16)
            read_sum = jnp.sum(read_k * khat, axis=1, keepdims=True)
            beta_col = jnp.sum(rhs_g * value + part_k, axis=1, keepdims=True) - grow * read_sum
            kept_sum = jnp.sum(kept_g * khat, axis=1, keepdims=True) * keep
            cumul_col = -(beta * grow) * read_sum + jnp.sum(gaps, axis=1, keepdims=True) - kept_sum
            whole = jnp.sum(back.astype(F32) * state.astype(F32)) * x.end[h]
            at_end = jnp.sum(kept_sum, axis=0, keepdims=True) + whole
            cumul_col += jnp.where(row[:, 0:1] == BLOCK - 1, at_end, 0.0)
            cumul_g = jnp.where(lane == h, cumul_col, cumul_g)
            beta_g = jnp.where(lane == h, beta_col, beta_g)
            across = jnp.where(level == h, jnp.sum(gaps, axis=0, keepdims=True), across)
        k_along = jnp.sum(khat * khat_g, axis=1, keepdims=True)
        dk_ref[0, :, cut] = (x.k_scale[j] * (khat_g - khat * k_along)).astype(BF16)
    db_ref[0] = beta_g.T
    dg_ref[0] = exact(part_dg_ref[0] + cumul_g.T - across, (row >= col).astype(F32))


def fetched(kernel, count, refs, scratch):
    *held, sems = scratch
    fetches = [pltpu.make_async_copy(refs[i], held[i], sems.at[i]) for i in range(count)]
    for copy in fetches:
        copy.start()
    for copy in fetches:
        copy.wait()
    kernel(*held)
    puts = [pltpu.make_async_copy(held[i], refs[i], sems.at[i]) for i in range(count, len(refs))]
    for copy in puts:
        copy.start()
    for copy in puts:
        copy.wait()


def query_gradients_on(turn, at_ref, *refs):
    outs = refs[8:16] if turn else refs[16:24]

    @pl.when(at_ref[0] == turn)
    def _():
        fetched(query_gradients, 7, (*refs[:7], *outs), refs[-16:])


def all_gradients(*refs):
    fetched(gradients, 15, refs[:19], refs[19:])


def whole(x):
    return pl.BlockSpec(x.shape, lambda *i: (0,) * len(x.shape))


SCALAR = pl.BlockSpec(memory_space=pltpu.SMEM)
HELD = pl.BlockSpec(memory_space=pltpu.VMEM)
FAR = pl.BlockSpec(memory_space=pl.ANY)


def call(kernel, outs, *args, ins=None, out_specs=None, flops=0, scratch=(), grid=(), limit=24, **more):
    size = sum(math.prod(x.shape) * x.dtype.itemsize for x in (*args, *outs))
    return pl.pallas_call(
        kernel,
        grid=grid,
        out_shape=outs,
        in_specs=[HELD] * len(args) if ins is None else ins,
        out_specs=[HELD] * len(outs) if out_specs is None else out_specs,
        scratch_shapes=scratch,
        compiler_params=pltpu.CompilerParams(vmem_limit_bytes=limit * 2**20),
        cost_estimate=pl.CostEstimate(flops=flops, bytes_accessed=size, transcendentals=0),
        **more,
    )(*args)


def shape(dims, dtype):
    return jax.ShapeDtypeStruct(dims, dtype)


def far(dims, dtype):
    return pltpu.HBM(dims, dtype)


def fixed(x):
    return pltpu.with_memory_space_constraint(x, pltpu.HBM)


def body(
    queries, key_rows, value_rows, log_decay, write_rate,
    initial_state, final_state_grad, output_matrix, output_grad,
):
    heads = log_decay.shape[1]
    blocks = lax.axis_size("ctx")
    feats = lax.axis_size("tp")
    here, core = lax.axis_index("ctx"), lax.axis_index("dp")
    rows, wide = output_matrix.shape
    piece = rows // blocks
    swap = [(0, 1), (1, 0)]
    square = (heads, BLOCK, DK)
    unit = 2 * BLOCK**3 * heads

    def halves(states):
        return fixed(states.reshape(blocks, HALF, DK))

    with jax.named_scope("gather_grad"):
        grads = [output_grad]
        for k in range(1, feats):
            pairs = [((i + k) % feats, i) for i in range(feats)]
            grads.append(lax.ppermute(output_grad, "tp", pairs))
    with jax.named_scope("other_rows"):
        other_matrix = lax.ppermute(output_matrix, "dp", swap)
    dma = pltpu.SemaphoreType.DMA
    with jax.named_scope("local_maps"):
        args = tuple(map(fixed, (queries, key_rows, value_rows, log_decay, write_rate)))
        outs = [far((blocks, DK + HALF, DK), BF16)] + [far(square, BF16)] * 2
        maps, qe, o0 = call(
            local_maps, outs, *args,
            ins=[FAR] * 5, out_specs=[FAR] * 3,
            scratch=[pltpu.VMEM(x.shape, x.dtype) for x in args]
            + [pltpu.VMEM((blocks, DK + HALF, DK), BF16)]
            + [pltpu.VMEM(square, BF16)] * 2
            + [dma((5,)), dma((2, 3))],
            flops=50 * unit,
        )
    with jax.named_scope("send_maps"):
        maps = lax.all_to_all(maps, "ctx", 0, 0, tiled=True)
    with jax.named_scope("head_grads"):
        place = jnp.stack([core, lax.axis_index("tp")])
        gather = pltpu.VMEM((feats,) + output_grad.shape[1:], BF16)
        backs, head_grad = call(
            head_grads,
            [far((blocks, HALF, DK), BF16), shape((BLOCK, wide), BF16)],
            place, *grads, fixed(output_matrix), other_matrix, fixed(qe),
            ins=[SCALAR] + [HELD] * feats + [FAR, HELD, FAR],
            out_specs=[FAR, HELD],
            scratch=[
                gather,
                pltpu.VMEM(output_matrix.shape, BF16),
                pltpu.VMEM(square, BF16),
                pltpu.VMEM((blocks, HALF, DK), BF16),
                dma((2,)),
                dma((2,)),
            ],
            flops=18 * unit,
        )
    with jax.named_scope("grad_rows"):
        mine, theirs = call(
            grad_rows, [shape((rows, BLOCK), BF16)] * 2, place, *grads,
            ins=[SCALAR] + [HELD] * feats, scratch=[gather],
        )
        theirs = lax.ppermute(theirs, "dp", swap)
    pieces = (blocks, piece, wide)
    buffer = far((blocks, piece, wide + DK), BF16)
    with jax.named_scope("forward_chain"):
        maps = fixed(maps)
        states, = call(
            forward_chain, [far((blocks, 2 * HALF, DK), BF16)],
            here.reshape(1), maps, fixed(backs), halves(initial_state),
            ins=[SCALAR] + [FAR] * 3, out_specs=[FAR],
            scratch=[
                pltpu.VMEM(maps.shape, BF16),
                pltpu.VMEM((blocks, 2 * HALF, DK), BF16),
                pltpu.VMEM((HALF, DK), F32),
                dma((2,)),
                dma((4,)),
                dma((4,)),
            ],
            flops=2 * unit,
        )
    with jax.named_scope("return_states"):
        states = lax.all_to_all(states, "ctx", 0, 0, tiled=True)
    with jax.named_scope("outputs"):
        heads_low, = call(
            outputs, [shape((BLOCK, wide), BF16)], qe, o0, states, flops=unit
        )
        other_low = lax.ppermute(heads_low, "dp", swap)
    with jax.named_scope("backward_chain"):
        partial, = call(
            backward_chain, [buffer], here.reshape(1), maps, states, halves(final_state_grad),
            ins=[SCALAR, FAR, HELD, FAR], out_specs=[FAR],
            scratch=[
                pltpu.VMEM((blocks, DK, DK), BF16),
                pltpu.VMEM((blocks, HALF, DK), BF16),
                pltpu.VMEM((HALF, DK), F32),
                dma(()),
                dma((4,)),
                dma((4,)),
            ],
            flops=2 * unit,
        )
    with jax.named_scope("projection"):
        partial, = call(
            projection, [buffer], mine, theirs, heads_low, other_low, fixed(partial),
            ins=[HELD] * 4 + [FAR], out_specs=[FAR],
            scratch=[pltpu.VMEM(pieces, BF16), dma((4,))], flops=16 * unit,
            input_output_aliases={4: 0},
        )

    def holding(*arrays):
        return [pltpu.VMEM(x.shape, x.dtype) for x in arrays] + [dma((len(arrays),))]

    with jax.named_scope("gradients"):
        args += (head_grad, states)
        results = [
            far(queries.shape, BF16), far(key_rows.shape, F32), far(log_decay.shape, F32),
            far(square, F32), *[far(square, BF16)] * 4,
        ]
        held = holding(*args, *results)
        *results, partial = call(
            functools.partial(query_gradients_on, 1), results + [buffer],
            core.reshape(1), *args, fixed(partial),
            ins=[SCALAR] + [FAR] * 8, out_specs=[FAR] * 9, scratch=held,
            flops=35 * unit, input_output_aliases={8: 8},
        )
    with jax.named_scope("projection"):
        partial = lax.all_to_all(partial, "ctx", 0, 0, tiled=True)
        spread, backs = call(
            functools.partial(reduce_spread, float(BLOCK * blocks * lax.axis_size("dp")) ** (-0.5)),
            [far(pieces, BF16), far((blocks, HALF, DK), BF16)], partial, out_specs=[FAR] * 2,
            scratch=[pltpu.VMEM((piece, wide), BF16), dma(()), dma((blocks, 2))],
        )
        total = lax.all_to_all(spread, "ctx", 0, 0, tiled=True).reshape(rows, wide)
        weight_grad, = call(
            widen, [far((rows, wide), F32)], total,
            out_specs=[FAR], scratch=[pltpu.VMEM((rows, wide), F32), dma((8,))],
        )
    with jax.named_scope("gradients"):
        results = call(
            functools.partial(query_gradients_on, 0), [far(x.shape, x.dtype) for x in results],
            core.reshape(1), *args, fixed(spread), *map(fixed, results),
            ins=[SCALAR] + [FAR] * 16, out_specs=[FAR] * 8, scratch=held,
            flops=35 * unit, input_output_aliases={9 + i: i for i in range(8)},
        )
        query_g, *shares = results
        outs = [far(x.shape, x.dtype) for x in args[1:5]]
        args += (fixed(backs), *map(fixed, shares))
        key_g, value_g, decay_g, rate_g = call(
            all_gradients, outs, *args,
            ins=[FAR] * 15, out_specs=[FAR] * 4, scratch=holding(*args, *outs),
            flops=35 * unit,
        )
    return (query_g, key_g, value_g, decay_g, rate_g, weight_grad)


def solution(mesh):
    rows = P("dp", "ctx", "tp")
    gates = P("dp", "tp", "ctx")
    state = P("dp", "tp", None, None)
    return jax.shard_map(
        body,
        mesh=mesh,
        in_specs=(rows, rows, rows, gates, gates, state, state, P("dp", "tp"), rows),
        out_specs=(rows, rows, rows, gates, gates, P("dp", "tp")),
        check_vma=False,
    )
```

```python
import functools
import math

import jax
import jax.numpy as jnp
from jax import lax
from jax.experimental import pallas as pl
from jax.experimental.pallas import tpu as pltpu
from jax.sharding import PartitionSpec as P

DK = 128
DV = 128
BLOCK = 128
HALF = DV // 2
F32 = jnp.float32
BF16 = jnp.bfloat16
QSCALE = DK ** (-0.5)

NN = (((1,), (0,)), ((), ()))
NT = (((1,), (1,)), ((), ()))
TN = (((0,), (0,)), ((), ()))


def mm(a, b, dims=NN):
    return lax.dot_general(a.astype(BF16), b.astype(BF16), dims, preferred_element_type=F32)


def split(a):
    high = a.astype(BF16)
    return high, (a - high.astype(F32)).astype(BF16)


def mm3(a, b, dims=NN):
    return mm(a[0], b[0], dims) + (mm(a[0], b[1], dims) + mm(a[1], b[0], dims))


def mm_left(a, b, dims=NN):
    low = b.astype(BF16)
    return mm(a[0], low, dims) + mm(a[1], low, dims)


def mm_right(a, b, dims=NN):
    low = a.astype(BF16)
    return mm(low, b[0], dims) + mm(low, b[1], dims)


def exact(a, b):
    return lax.dot_general(
        a, b, NN, precision=lax.Precision.HIGHEST, preferred_element_type=F32
    )


def iotas():
    row = lax.broadcasted_iota(jnp.int32, (BLOCK, BLOCK), 0)
    col = lax.broadcasted_iota(jnp.int32, (BLOCK, BLOCK), 1)
    return row, col


def unit_rows(rows):
    scale = lax.rsqrt(jnp.sum(rows * rows, axis=-1, keepdims=True) + 1e-06)
    return rows * scale, scale


def gate_columns(gates, row, col):
    cumul = exact(gates, (row <= col).astype(F32))
    columns = cumul.T
    last = columns[BLOCK - 1 : BLOCK, :]
    return cumul, columns, jnp.exp(columns), jnp.exp(last - columns), jnp.exp(last)


def decays(cumul, columns, h, strict):
    gap = columns[:, h : h + 1] - cumul[h : h + 1, :]
    return jnp.where(strict, jnp.exp(jnp.where(strict, gap, 0.0)), 0.0)


def unit_lower_inverses(parts, row, col, finer):
    ident = (row == col).astype(F32)
    found = None
    size = 1
    while size < BLOCK:
        off = (row // (2 * size) == col // (2 * size)) & (row // size != col // size)
        offs = [jnp.where(off, a, 0.0) for a in parts]
        if size == 1:
            found = [ident - a for a in offs]
        else:
            lows = [t.astype(BF16) for t in found]
            inner = [mm(t, a) for t, a in zip(lows, offs)]
            found = [t - mm(x, s) for t, x, s in zip(found, inner, lows)]
        size *= 2
    lows = [t.astype(BF16) for t in found]
    rest = [ident - (t.astype(F32) + mm_left(split(a), t)) for t, a in zip(lows, parts)]
    found = [t.astype(F32) + mm(t, r) for t, r in zip(lows, rest)]
    if finer:
        rest = [ident - (t + mm3(split(a), split(t))) for t, a in zip(found, parts)]
        found = [t + mm3(split(t), split(r)) for t, r in zip(found, rest)]
    return found


class Heads:
    def __init__(self, q_ref, k_ref, g_ref, b_ref, inverse=None, finer=False):
        self.count = g_ref.shape[1]
        self.copies = self.count * DK // q_ref.shape[2]
        self.row, self.col = iotas()
        self.ident = (self.row == self.col).astype(F32)
        strict = self.row > self.col
        cumul, columns, growth, weight, ends = gate_columns(g_ref[0], self.row, self.col)
        betas = b_ref[0].T
        one = [slice(h, h + 1) for h in range(self.count)]
        self.decay = [decays(cumul, columns, h, strict) for h in range(self.count)]
        self.beta, self.grow, self.keep, self.end = (
            [x[:, cut] for cut in one] for x in (betas, growth, weight, ends)
        )
        self.qn, self.q_scale, self.khat, self.k_scale = [], [], [], []
        self.pair_k, self.pair_q = [], []
        for j in range(self.count // self.copies):
            cut = slice(j * DK, (j + 1) * DK)
            qn, q_scale = unit_rows(q_ref[0, :, cut].astype(F32))
            khat, k_scale = unit_rows(k_ref[0, :, cut].astype(F32))
            self.qn.append(qn)
            self.q_scale.append(q_scale)
            self.khat.append(khat)
            self.k_scale.append(k_scale)
            self.pair_k.append(mm(khat, khat, NT))
            self.pair_q.append(mm(qn * QSCALE, khat, NT))
        self.inverse = inverse
        if inverse is None:
            parts = [
                self.beta[h] * self.pair_k[h // self.copies] * self.decay[h]
                for h in range(self.count)
            ]
            found = unit_lower_inverses(parts, self.row, self.col, finer)
            self.inverse = [split(t) for t in found]

    def fresh(self, h, value, state):
        read = mm_left(split(self.khat[h // self.copies]), state, NT)
        return split(mm3(self.inverse[h], split(self.beta[h] * (value - self.grow[h] * read))))


def local_maps(*refs):
    far_in, far_out, held, kept, in_sems, out_sems = (
        refs[:5], refs[5:8], refs[8:13], refs[13:16], *refs[16:]
    )
    fetches = [pltpu.make_async_copy(far_in[i], held[i], in_sems.at[i]) for i in range(5)]
    for copy in fetches:
        copy.start()
    for copy in fetches:
        copy.wait()
    q_ref, k_ref, v_ref, g_ref, b_ref = held
    pay_ref, qe_ref, o0_ref = kept
    x = Heads(q_ref, k_ref, g_ref, b_ref)
    parts = out_sems.shape[0]
    some = x.count // parts
    puts = []
    for h in range(x.count):
        j = h // x.copies
        value = v_ref[0, :, h * DV : (h + 1) * DV].astype(F32)
        wm = mm_left(x.inverse[h], (x.beta[h] * x.grow[h]) * x.khat[j])
        u0 = mm_left(x.inverse[h], x.beta[h] * value)
        kw = split(x.keep[h] * x.khat[j])
        step = (x.end[h] * x.ident - mm_right(wm, kw, TN)).astype(BF16)
        write = mm_right(u0, kw, TN).astype(BF16)
        scores = x.pair_q[j] * (x.decay[h] + x.ident)
        qe_ref[h] = (x.grow[h] * (x.qn[j] * QSCALE) - mm(scores, wm)).astype(BF16)
        o0_ref[h] = mm(scores, u0).astype(BF16)
        for half in range(2):
            pay_ref[2 * h + half, 0:DK] = step
            pay_ref[2 * h + half, DK:] = write[half * HALF : (half + 1) * HALF]
        if (h + 1) % some == 0:
            p, at = h // some, pl.ds(h + 1 - some, some)
            both = pl.ds(2 * (h + 1 - some), 2 * some)
            moves = (
                (pay_ref.at[both], far_out[0].at[both]),
                (qe_ref.at[at], far_out[1].at[at]),
                (o0_ref.at[at], far_out[2].at[at]),
            )
            for i, (a, b) in enumerate(moves):
                puts.append(pltpu.make_async_copy(a, b, out_sems.at[p, i]))
                puts[-1].start()
    for copy in puts:
        copy.wait()


def gathered_into(all_ref, here, refs):
    for k, ref in enumerate(refs):
        all_ref[lax.rem(here + k, all_ref.shape[0])] = ref[0]


def head_grads(
    at_ref, g0_ref, g1_ref, g2_ref, g3_ref, own_hbm, other_ref, qe_hbm,
    back_out, hg_ref, all_ref, own_ref, qe_ref, back_ref, in_sems, out_sems,
):
    fetch = pltpu.make_async_copy(own_hbm, own_ref, in_sems.at[0])
    fetch_qe = pltpu.make_async_copy(qe_hbm, qe_ref, in_sems.at[1])
    fetch.start()
    fetch_qe.start()
    core, here = at_ref[0], at_ref[1]
    gathered_into(all_ref, here, (g0_ref, g1_ref, g2_ref, g3_ref))
    feats, wide = all_ref.shape[0], all_ref.shape[2]
    half = feats // 2
    total = jnp.zeros((BLOCK, own_ref.shape[1]), F32)
    for i in range(half):
        total += mm(all_ref[half * (1 - core) + i], other_ref[i * wide : (i + 1) * wide, :])
    fetch.wait()
    for i in range(half):
        total += mm(all_ref[half * core + i], own_ref[i * wide : (i + 1) * wide, :])
    total = total.astype(BF16)
    hg_ref[...] = total
    fetch_qe.wait()
    parts = out_sems.shape[0]
    some = qe_ref.shape[0] // parts
    puts = []
    for p in range(parts):
        for h in range(p * some, (p + 1) * some):
            back = mm(total[:, h * DV : (h + 1) * DV], qe_ref[h], TN).astype(BF16)
            for side in range(2):
                back_ref[2 * h + side] = back[side * HALF : (side + 1) * HALF]
        at = pl.ds(2 * p * some, 2 * some)
        puts.append(pltpu.make_async_copy(back_ref.at[at], back_out.at[at], out_sems.at[p]))
        puts[-1].start()
    for copy in puts:
        copy.wait()


def grad_rows(at_ref, g0_ref, g1_ref, g2_ref, g3_ref, mine_ref, theirs_ref, all_ref):
    core, here = at_ref[0], at_ref[1]
    gathered_into(all_ref, here, (g0_ref, g1_ref, g2_ref, g3_ref))
    feats, wide = all_ref.shape[0], all_ref.shape[2]
    half = feats // 2
    for i in range(half):
        cut = slice(i * wide, (i + 1) * wide)
        mine_ref[cut, :] = all_ref[half * core + i].T
        theirs_ref[cut, :] = all_ref[half * (1 - core) + i].T


def times(state, step, dims):
    out = mm(jnp.concatenate(split(state), axis=0), step, dims)
    return out[:HALF] + out[HALF:]


def forward_chain(
    at_ref, maps_hbm, back_hbm, first_hbm, out_ref,
    maps_ref, kept_ref, first_ref, back_sems, in_sems, sems,
):
    blocks, parts = maps_ref.shape[0], sems.shape[0]
    some = blocks // parts
    groups = [pl.ds(p * some, some) for p in range(parts)]
    fetches = [
        pltpu.make_async_copy(maps_hbm.at[at], maps_ref.at[at], in_sems.at[p])
        for p, at in enumerate(groups)
    ]
    fetch_first = pltpu.make_async_copy(first_hbm.at[at_ref[0]], first_ref, back_sems.at[1])
    fetch_first.start()
    fetches[0].start()
    fetch_back = pltpu.make_async_copy(back_hbm, kept_ref.at[:, pl.ds(HALF, HALF)], back_sems.at[0])
    fetch_back.start()
    for copy in fetches[1:]:
        copy.start()
    copies = []
    fetch_first.wait()
    state = first_ref[...]
    for c in range(blocks):
        kept_ref[c, 0:HALF] = state.astype(BF16)
        if c % some == 0:
            fetches[c // some].wait()
        if (c + 1) % some == 0:
            p = c // some
            if p == 0:
                fetch_back.wait()
            at = groups[p]
            copies.append(pltpu.make_async_copy(kept_ref.at[at], out_ref.at[at], sems.at[p]))
            copies[-1].start()
        if c < blocks - 1:
            state = times(state, maps_ref[c, 0:DK], NN) + maps_ref[c, DK:].astype(F32)
    for copy in copies:
        copy.wait()


def backward_chain(
    at_ref, maps_hbm, in_ref, last_hbm, out_ref, maps_ref, kept_ref, last_ref, last_sem, in_sems, sems
):
    blocks, parts = maps_ref.shape[0], sems.shape[0]
    some = blocks // parts
    wide = out_ref.shape[2] - DK
    groups = [pl.ds(p * some, some) for p in range(parts)]
    fetches = [
        pltpu.make_async_copy(maps_hbm.at[at, pl.ds(0, DK)], maps_ref.at[at], in_sems.at[p])
        for p, at in enumerate(groups)
    ]
    fetch_last = pltpu.make_async_copy(last_hbm.at[at_ref[0]], last_ref, last_sem)
    fetch_last.start()
    for copy in reversed(fetches):
        copy.start()
    copies = []
    fetch_last.wait()
    back = last_ref[...]
    for c in range(blocks - 1, -1, -1):
        kept_ref[c] = back.astype(BF16)
        p = c // some
        if c % some == some - 1:
            fetches[p].wait()
        if c % some == 0:
            out = out_ref.at[groups[p], :, pl.ds(wide, DK)]
            copies.append(pltpu.make_async_copy(kept_ref.at[groups[p]], out, sems.at[p]))
            copies[-1].start()
        if c > 0:
            back = times(back, maps_ref[c], NT) + in_ref[c, HALF:].astype(F32)
    for copy in copies:
        copy.wait()


def projection(mine_ref, theirs_ref, low_ref, other_ref, in_ref, out_ref, kept_ref, sems):
    blocks, piece, wide = kept_ref.shape
    parts = sems.shape[0]
    some = blocks // parts
    lows = jnp.concatenate([low_ref[...], other_ref[...]], axis=0)
    copies = []
    for p in range(parts):
        cut = slice(p * some * piece, (p + 1) * some * piece)
        rows = jnp.concatenate([mine_ref[cut, :], theirs_ref[cut, :]], axis=1)
        total = mm(rows, lows).astype(BF16)
        for c in range(some):
            kept_ref[p * some + c] = total[c * piece : (c + 1) * piece]
        at = pl.ds(p * some, some)
        out = out_ref.at[at, :, pl.ds(0, wide)]
        copies.append(pltpu.make_async_copy(kept_ref.at[at], out, sems.at[p]))
        copies[-1].start()
    for copy in copies:
        copy.wait()


def reduce_spread(scale, pieces_ref, out_ref, back_ref, sum_ref, back_sem, sems):
    blocks, rows, wide = out_ref.shape
    parts = sems.shape[1]
    copies = []
    for p in range(parts):
        at = pl.ds(p * (rows // parts), rows // parts)
        total = pieces_ref[0, at, 0:wide].astype(F32)
        for c in range(1, blocks):
            total += pieces_ref[c, at, 0:wide].astype(F32)
        sum_ref[at] = (total * scale).astype(BF16)
        for c in range(blocks):
            copy = pltpu.make_async_copy(sum_ref.at[at], out_ref.at[c, at], sems.at[c, p])
            copy.start()
            copies.append(copy)
    back = pieces_ref.at[:, :, pl.ds(wide, DK)]
    copies.append(pltpu.make_async_copy(back, back_ref, back_sem))
    copies[-1].start()
    for copy in copies:
        copy.wait()


def widen(in_ref, out_ref, kept_ref, sems):
    parts = sems.shape[0]
    step = in_ref.shape[0] // parts
    copies = []
    for p in range(parts):
        at = pl.ds(p * step, step)
        kept_ref[at, :] = in_ref[at, :].astype(F32)
        copies.append(pltpu.make_async_copy(kept_ref.at[at], out_ref.at[at], sems.at[p]))
        copies[-1].start()
    for copy in copies:
        copy.wait()


def halves_of(ref, h, low):
    rows = slice(low, low + HALF)
    return jnp.concatenate([ref[2 * h, rows], ref[2 * h + 1, rows]], axis=0)


def outputs(qe_ref, o0_ref, y_ref, o_ref):
    for h in range(qe_ref.shape[0]):
        out = o0_ref[h].astype(F32) + mm(qe_ref[h], halves_of(y_ref, h, 0), NT)
        o_ref[:, h * DV : (h + 1) * DV] = out.astype(BF16)


def query_gradients(
    q_ref, k_ref, v_ref, g_ref, b_ref, hg_ref, y_ref, dq_ref, dk_ref, dg_ref, rhs_ref,
    *kept_refs,
):
    x = Heads(q_ref, k_ref, g_ref, b_ref, finer=True)
    lane = lax.broadcasted_iota(jnp.int32, (BLOCK, x.count), 1)
    level = lax.broadcasted_iota(jnp.int32, (x.count, BLOCK), 0)
    cumul_g = jnp.zeros((BLOCK, x.count), F32)
    across = jnp.zeros((x.count, BLOCK), F32)
    for j in range(x.count // x.copies):
        cut = slice(j * DK, (j + 1) * DK)
        qn, klow = x.qn[j], x.khat[j].astype(BF16)
        qhat = qn * QSCALE
        qlow = qhat.astype(BF16)
        qhat_g = jnp.zeros((BLOCK, DK), F32)
        khat_g = jnp.zeros((BLOCK, DK), F32)
        for h in range(j * x.copies, (j + 1) * x.copies):
            cut_v = slice(h * DV, (h + 1) * DV)
            value = v_ref[0, :, cut_v].astype(F32)
            state, out_g = halves_of(y_ref, h, 0), hg_ref[:, cut_v]
            decay_in = x.decay[h] + x.ident
            fresh = x.fresh(h, value, state)
            for ref, part in zip(kept_refs, (*x.inverse[h], *fresh)):
                ref[h] = part
            pair_g = mm_right(out_g, fresh, NT) * decay_in
            gaps = pair_g * x.pair_q[j]
            pair_g = split(pair_g)
            scores = x.pair_q[j] * decay_in
            fresh_g = mm_left(split(scores), out_g, TN)
            rhs_ref[h] = mm3(x.inverse[h], split(fresh_g), TN)
            read_q = mm(out_g, state)
            low_q, low_k = mm_left(pair_g, klow), mm_left(pair_g, qlow, TN)
            qhat_g += x.grow[h] * read_q + low_q.astype(BF16).astype(F32)
            khat_g += low_k.astype(BF16).astype(F32)
            grow_g = jnp.sum(read_q * qhat, axis=1, keepdims=True)
            cumul_col = grow_g * x.grow[h] + jnp.sum(gaps, axis=1, keepdims=True)
            cumul_g = jnp.where(lane == h, cumul_col, cumul_g)
            across = jnp.where(level == h, jnp.sum(gaps, axis=0, keepdims=True), across)
        q_along = jnp.sum(qn * qhat_g, axis=1, keepdims=True)
        dq_ref[0, :, cut] = ((x.q_scale[j] * QSCALE) * (qhat_g - qn * q_along)).astype(BF16)
        dk_ref[0, :, cut] = khat_g
    dg_ref[0] = cumul_g.T - across


def gradients(
    q_ref, k_ref, v_ref, g_ref, b_ref, hg_ref, y_ref, back_ref, part_dk_ref, part_dg_ref,
    part_rhs_ref, t_high_ref, t_low_ref, fresh_high_ref, fresh_low_ref,
    dk_ref, dv_ref, dg_ref, db_ref,
):
    inverse = [(t_high_ref[h], t_low_ref[h]) for h in range(g_ref.shape[1])]
    x = Heads(q_ref, k_ref, g_ref, b_ref, inverse)
    row, col = x.row, x.col
    strict = row > col
    lane = lax.broadcasted_iota(jnp.int32, (BLOCK, x.count), 1)
    level = lax.broadcasted_iota(jnp.int32, (x.count, BLOCK), 0)
    cumul_g = jnp.zeros((BLOCK, x.count), F32)
    beta_g = jnp.zeros((BLOCK, x.count), F32)
    across = jnp.zeros((x.count, BLOCK), F32)
    for j in range(x.count // x.copies):
        cut = slice(j * DK, (j + 1) * DK)
        khat = x.khat[j]
        klow = khat.astype(BF16)
        pair_k = x.pair_k[j]
        khat_g = part_dk_ref[0, :, cut]
        for h in range(j * x.copies, (j + 1) * x.copies):
            cut_v = slice(h * DV, (h + 1) * DV)
            decay, grow, keep, beta = x.decay[h], x.grow[h], x.keep[h], x.beta[h]
            value = v_ref[0, :, cut_v].astype(F32)
            state, back = halves_of(y_ref, h, 0), halves_of(back_ref, h, 0)
            fresh = fresh_high_ref[h], fresh_low_ref[h]
            fresh_g = mm_left(split(keep * khat), back, NT)
            rhs_g = part_rhs_ref[h] + mm3(x.inverse[h], split(fresh_g), TN)
            rhs = split(rhs_g)
            read_k = mm_left(rhs, state)
            part_g = jnp.where(strict, -mm3(rhs, fresh, NT), 0.0) * decay
            pair_kg = split(part_g * beta)
            kept_g = mm_left(fresh, back)
            part_k = part_g * pair_k
            gaps = part_k * beta
            low_k = mm_left(pair_kg, klow) + mm_left(pair_kg, klow, TN)
            khat_g += keep * kept_g - (beta * grow) * read_k + low_k.astype(BF16).astype(F32)
            dv_ref[0, :, cut_v] = (beta * rhs_g).astype(BF16)
            read_sum = jnp.sum(read_k * khat, axis=1, keepdims=True)
            beta_col = jnp.sum(rhs_g * value + part_k, axis=1, keepdims=True) - grow * read_sum
            kept_sum = jnp.sum(kept_g * khat, axis=1, keepdims=True) * keep
            cumul_col = -(beta * grow) * read_sum + jnp.sum(gaps, axis=1, keepdims=True) - kept_sum
            whole = jnp.sum(back.astype(F32) * state.astype(F32)) * x.end[h]
            at_end = jnp.sum(kept_sum, axis=0, keepdims=True) + whole
            cumul_col += jnp.where(row[:, 0:1] == BLOCK - 1, at_end, 0.0)
            cumul_g = jnp.where(lane == h, cumul_col, cumul_g)
            beta_g = jnp.where(lane == h, beta_col, beta_g)
            across = jnp.where(level == h, jnp.sum(gaps, axis=0, keepdims=True), across)
        k_along = jnp.sum(khat * khat_g, axis=1, keepdims=True)
        dk_ref[0, :, cut] = (x.k_scale[j] * (khat_g - khat * k_along)).astype(BF16)
    db_ref[0] = beta_g.T
    dg_ref[0] = exact(part_dg_ref[0] + cumul_g.T - across, (row >= col).astype(F32))


def fetched(kernel, count, refs, scratch):
    *held, sems = scratch
    fetches = [pltpu.make_async_copy(refs[i], held[i], sems.at[i]) for i in range(count)]
    for copy in fetches:
        copy.start()
    for copy in fetches:
        copy.wait()
    kernel(*held)
    puts = [pltpu.make_async_copy(held[i], refs[i], sems.at[i]) for i in range(count, len(refs))]
    for copy in puts:
        copy.start()
    for copy in puts:
        copy.wait()


def query_gradients_on(turn, at_ref, *refs):
    outs = refs[8:16] if turn else refs[16:24]

    @pl.when(at_ref[0] == turn)
    def _():
        fetched(query_gradients, 7, (*refs[:7], *outs), refs[-16:])


def all_gradients(*refs):
    fetched(gradients, 15, refs[:19], refs[19:])


def whole(x):
    return pl.BlockSpec(x.shape, lambda *i: (0,) * len(x.shape))


SCALAR = pl.BlockSpec(memory_space=pltpu.SMEM)
HELD = pl.BlockSpec(memory_space=pltpu.VMEM)
FAR = pl.BlockSpec(memory_space=pl.ANY)


def call(kernel, outs, *args, ins=None, out_specs=None, flops=0, scratch=(), grid=(), limit=24, **more):
    size = sum(math.prod(x.shape) * x.dtype.itemsize for x in (*args, *outs))
    return pl.pallas_call(
        kernel,
        grid=grid,
        out_shape=outs,
        in_specs=[HELD] * len(args) if ins is None else ins,
        out_specs=[HELD] * len(outs) if out_specs is None else out_specs,
        scratch_shapes=scratch,
        compiler_params=pltpu.CompilerParams(vmem_limit_bytes=limit * 2**20),
        cost_estimate=pl.CostEstimate(flops=flops, bytes_accessed=size, transcendentals=0),
        **more,
    )(*args)


def shape(dims, dtype):
    return jax.ShapeDtypeStruct(dims, dtype)


def far(dims, dtype):
    return pltpu.HBM(dims, dtype)


def fixed(x):
    return pltpu.with_memory_space_constraint(x, pltpu.HBM)


def body(
    queries, key_rows, value_rows, log_decay, write_rate,
    initial_state, final_state_grad, output_matrix, output_grad,
):
    heads = log_decay.shape[1]
    blocks = lax.axis_size("ctx")
    feats = lax.axis_size("tp")
    here, core = lax.axis_index("ctx"), lax.axis_index("dp")
    rows, wide = output_matrix.shape
    piece = rows // blocks
    swap = [(0, 1), (1, 0)]
    square = (heads, BLOCK, DK)
    unit = 2 * BLOCK**3 * heads

    def halves(states):
        return fixed(states.reshape(blocks, HALF, DK))

    with jax.named_scope("gather_grad"):
        grads = [output_grad]
        for k in range(1, feats):
            pairs = [((i + k) % feats, i) for i in range(feats)]
            grads.append(lax.ppermute(output_grad, "tp", pairs))
    with jax.named_scope("other_rows"):
        other_matrix = lax.ppermute(output_matrix, "dp", swap)
    dma = pltpu.SemaphoreType.DMA
    with jax.named_scope("local_maps"):
        args = tuple(map(fixed, (queries, key_rows, value_rows, log_decay, write_rate)))
        outs = [far((blocks, DK + HALF, DK), BF16)] + [far(square, BF16)] * 2
        maps, qe, o0 = call(
            local_maps, outs, *args,
            ins=[FAR] * 5, out_specs=[FAR] * 3,
            scratch=[pltpu.VMEM(x.shape, x.dtype) for x in args]
            + [pltpu.VMEM((blocks, DK + HALF, DK), BF16)]
            + [pltpu.VMEM(square, BF16)] * 2
            + [dma((5,)), dma((2, 3))],
            flops=50 * unit,
        )
    with jax.named_scope("send_maps"):
        maps = lax.all_to_all(maps, "ctx", 0, 0, tiled=True)
    with jax.named_scope("head_grads"):
        place = jnp.stack([core, lax.axis_index("tp")])
        gather = pltpu.VMEM((feats,) + output_grad.shape[1:], BF16)
        backs, head_grad = call(
            head_grads,
            [far((blocks, HALF, DK), BF16), shape((BLOCK, wide), BF16)],
            place, *grads, fixed(output_matrix), other_matrix, fixed(qe),
            ins=[SCALAR] + [HELD] * feats + [FAR, HELD, FAR],
            out_specs=[FAR, HELD],
            scratch=[
                gather,
                pltpu.VMEM(output_matrix.shape, BF16),
                pltpu.VMEM(square, BF16),
                pltpu.VMEM((blocks, HALF, DK), BF16),
                dma((2,)),
                dma((2,)),
            ],
            flops=18 * unit,
        )
    with jax.named_scope("grad_rows"):
        mine, theirs = call(
            grad_rows, [shape((rows, BLOCK), BF16)] * 2, place, *grads,
            ins=[SCALAR] + [HELD] * feats, scratch=[gather],
        )
        theirs = lax.ppermute(theirs, "dp", swap)
    pieces = (blocks, piece, wide)
    buffer = far((blocks, piece, wide + DK), BF16)
    with jax.named_scope("forward_chain"):
        maps = fixed(maps)
        states, = call(
            forward_chain, [far((blocks, 2 * HALF, DK), BF16)],
            here.reshape(1), maps, fixed(backs), halves(initial_state),
            ins=[SCALAR] + [FAR] * 3, out_specs=[FAR],
            scratch=[
                pltpu.VMEM(maps.shape, BF16),
                pltpu.VMEM((blocks, 2 * HALF, DK), BF16),
                pltpu.VMEM((HALF, DK), F32),
                dma((2,)),
                dma((4,)),
                dma((4,)),
            ],
            flops=2 * unit,
        )
    with jax.named_scope("return_states"):
        states = lax.all_to_all(states, "ctx", 0, 0, tiled=True)
    with jax.named_scope("outputs"):
        heads_low, = call(
            outputs, [shape((BLOCK, wide), BF16)], qe, o0, states, flops=unit
        )
        other_low = lax.ppermute(heads_low, "dp", swap)
    with jax.named_scope("backward_chain"):
        partial, = call(
            backward_chain, [buffer], here.reshape(1), maps, states, halves(final_state_grad),
            ins=[SCALAR, FAR, HELD, FAR], out_specs=[FAR],
            scratch=[
                pltpu.VMEM((blocks, DK, DK), BF16),
                pltpu.VMEM((blocks, HALF, DK), BF16),
                pltpu.VMEM((HALF, DK), F32),
                dma(()),
                dma((4,)),
                dma((4,)),
            ],
            flops=2 * unit,
        )
    with jax.named_scope("projection"):
        partial, = call(
            projection, [buffer], mine, theirs, heads_low, other_low, fixed(partial),
            ins=[HELD] * 4 + [FAR], out_specs=[FAR],
            scratch=[pltpu.VMEM(pieces, BF16), dma((8,))], flops=16 * unit,
            input_output_aliases={4: 0},
        )

    def holding(*arrays):
        return [pltpu.VMEM(x.shape, x.dtype) for x in arrays] + [dma((len(arrays),))]

    with jax.named_scope("gradients"):
        args += (head_grad, states)
        results = [
            far(queries.shape, BF16), far(key_rows.shape, F32), far(log_decay.shape, F32),
            far(square, F32), *[far(square, BF16)] * 4,
        ]
        held = holding(*args, *results)
        *results, partial = call(
            functools.partial(query_gradients_on, 1), results + [buffer],
            core.reshape(1), *args, fixed(partial),
            ins=[SCALAR] + [FAR] * 8, out_specs=[FAR] * 9, scratch=held,
            flops=35 * unit, input_output_aliases={8: 8},
        )
    with jax.named_scope("projection"):
        partial = lax.all_to_all(partial, "ctx", 0, 0, tiled=True)
        spread, backs = call(
            functools.partial(reduce_spread, float(BLOCK * blocks * lax.axis_size("dp")) ** (-0.5)),
            [far(pieces, BF16), far((blocks, HALF, DK), BF16)], partial, out_specs=[FAR] * 2,
            scratch=[pltpu.VMEM((piece, wide), BF16), dma(()), dma((blocks, 2))],
        )
        total = lax.all_to_all(spread, "ctx", 0, 0, tiled=True).reshape(rows, wide)
        weight_grad, = call(
            widen, [far((rows, wide), F32)], total,
            out_specs=[FAR], scratch=[pltpu.VMEM((rows, wide), F32), dma((8,))],
        )
    with jax.named_scope("gradients"):
        results = call(
            functools.partial(query_gradients_on, 0), [far(x.shape, x.dtype) for x in results],
            core.reshape(1), *args, fixed(spread), *map(fixed, results),
            ins=[SCALAR] + [FAR] * 16, out_specs=[FAR] * 8, scratch=held,
            flops=35 * unit, input_output_aliases={9 + i: i for i in range(8)},
        )
        query_g, *shares = results
        outs = [far(x.shape, x.dtype) for x in args[1:5]]
        args += (fixed(backs), *map(fixed, shares))
        key_g, value_g, decay_g, rate_g = call(
            all_gradients, outs, *args,
            ins=[FAR] * 15, out_specs=[FAR] * 4, scratch=holding(*args, *outs),
            flops=35 * unit,
        )
    return (query_g, key_g, value_g, decay_g, rate_g, weight_grad)


def solution(mesh):
    rows = P("dp", "ctx", "tp")
    gates = P("dp", "tp", "ctx")
    state = P("dp", "tp", None, None)
    return jax.shard_map(
        body,
        mesh=mesh,
        in_specs=(rows, rows, rows, gates, gates, state, state, P("dp", "tp"), rows),
        out_specs=(rows, rows, rows, gates, gates, P("dp", "tp")),
        check_vma=False,
    )
```
